32 devices in a mesh: wide: 16 (over z, x, core), narrow: 2 (over y).
Axes of the slice: x: 2, y: 2, z: 4, core: 2. Of those that a mesh axis runs over, the one named last changes fastest.
Arguments:
- charges: float32 [64, 65536], P(None, ('wide', 'narrow')), may hold values from -6 to 6
- leaf_angle: float32 [64, 4096], P(None, ('wide', 'narrow')), may hold values from -3.140625 to 3.140625
- lagrange: float32 [48, 64], replicated, may hold values from -0.75 to 0.75
- level_angle: float32 [2, 48, 4096], P(None, None, ('wide', 'narrow')), may hold values from -3.140625 to 3.140625
- level_self: float32 [2, 96, 96], replicated, may hold values from -0.4375 to 0.4375
- level_peer: float32 [2, 96, 96], replicated, may hold values from -0.4375 to 0.4375
- switch_angle: float32 [48, 4096], P(None, ('wide', 'narrow')), may hold values from -3.140625 to 3.140625
- switch_matrix: float32 [96, 96], replicated, may hold values from -0.625 to 0.625
- out_angle: float32 [64, 4096], P(None, ('wide', 'narrow')), may hold values from -3.140625 to 3.140625
- evaluate: float32 [64, 48], replicated, may hold values from -0.875 to 0.875
Outputs:
- field: bfloat16 [64, 65536], P(None, ('wide', 'narrow'))
The draws below stay inside these ranges and needn't reach their ends.
All inputs are finite; a program needn't handle non-finite values.
Results may differ from the reference program's by a relative error of at most 0.0049.
Values may be sent and summed in bfloat16 or wider, within the bound.
A program may use at most 64 MiB of HBM per device.

```python
import jax
import jax.numpy as jnp
from jax import lax

K = 48
NRHS = 16
Q = 64
BOXES = 4096
COLUMNS = 65536
N_WIDE = 16
N_NARROW = 2


def level_of(stream_key, dims, shards, least, largest):
    gain, own = 1.0, jax.random.fold_in(stream_key, 6)
    for dim, blocks in shards:
        heights = jnp.exp(jax.random.uniform(jax.random.fold_in(own, dim), (blocks,), jnp.float32, least / len(shards), largest / len(shards)))
        gain = gain * jnp.repeat(heights, dims[dim] // blocks).reshape([-1 if axis == dim else 1 for axis in range(len(dims))])
    return gain


def scatter_about(key, extent, spread, bound, split=(), held_as=jnp.bfloat16):
    drawn = spread * jax.random.normal(key, extent, jnp.float32)
    if split:
        drawn = drawn * level_of(key, extent, split, -0.22, 0.18)
    return jnp.clip(drawn, -bound, bound).astype(held_as)


def setup_inputs(seed: int = 0) -> dict:
    keys = jax.random.split(jax.random.key(seed), 11)
    return {
        "charges": scatter_about(keys[0], (Q, COLUMNS), 1.0, 6.0, ((1, 32),), jnp.float32),
        "leaf_angle": jnp.clip(jax.random.uniform(keys[1], (Q, BOXES), jnp.float32, -3.140625, 3.140625), -3.140625, 3.140625),
        "lagrange": scatter_about(keys[2], (K, Q), Q ** -0.5, 0.75, (), jnp.float32),
        "level_angle": jnp.clip(jax.random.uniform(keys[3], (2, K, BOXES), jnp.float32, -3.140625, 3.140625), -3.140625, 3.140625),
        "level_self": scatter_about(keys[4], (2, 2 * K, 2 * K), (4 * K) ** -0.5, 0.4375, (), jnp.float32),
        "level_peer": scatter_about(keys[5], (2, 2 * K, 2 * K), (4 * K) ** -0.5, 0.4375, (), jnp.float32),
        "switch_angle": jnp.clip(jax.random.uniform(keys[6], (K, BOXES), jnp.float32, -3.140625, 3.140625), -3.140625, 3.140625),
        "switch_matrix": scatter_about(keys[7], (2 * K, 2 * K), (2 * K) ** -0.5, 0.625, (), jnp.float32),
        "out_angle": jnp.clip(jax.random.uniform(keys[8], (Q, BOXES), jnp.float32, -3.140625, 3.140625), -3.140625, 3.140625),
        "evaluate": scatter_about(keys[9], (Q, K), K ** -0.5, 0.875, (), jnp.float32),
    }


def product(left, right):
    return jnp.dot(left, right, precision=lax.Precision.HIGHEST, preferred_element_type=jnp.float32)


def rotate(boxes_state, phase_angle, per_box):
    rank = phase_angle.shape[0]
    cos_part = jnp.repeat(jnp.cos(phase_angle), per_box, axis=1)
    sin_part = jnp.repeat(jnp.sin(phase_angle), per_box, axis=1)
    real_part = boxes_state[:rank]
    imag_part = boxes_state[rank:]
    return jnp.concatenate([cos_part * real_part - sin_part * imag_part, sin_part * real_part + cos_part * imag_part], axis=0)


def partner_state(boxes_state, bit):
    rows = boxes_state.shape[0]
    view = boxes_state.reshape(rows, N_WIDE, N_NARROW >> (bit + 1), 2, 1 << bit, -1)
    return jnp.flip(view, 3).reshape(boxes_state.shape)


def butterfly_level(boxes_state, self_matrix, peer_matrix, phase_angle, bit, per_box):
    rounded = lax.optimization_barrier(partner_state(boxes_state, bit).astype(jnp.bfloat16))
    combined = product(self_matrix, boxes_state) + product(peer_matrix, rounded.astype(jnp.float32))
    return rotate(combined, phase_angle, per_box)


def reference(charges, leaf_angle, lagrange, level_angle, level_self, level_peer, switch_angle, switch_matrix, out_angle, evaluate):
    per_box = NRHS
    rank = lagrange.shape[0]
    cos_leaf = jnp.repeat(jnp.cos(leaf_angle), per_box, axis=1)
    sin_leaf = jnp.repeat(jnp.sin(leaf_angle), per_box, axis=1)
    boxes_state = jnp.concatenate([product(lagrange, cos_leaf * charges), product(lagrange, sin_leaf * charges)], axis=0)
    boxes_state = butterfly_level(boxes_state, level_self[0], level_peer[0], level_angle[0], 0, per_box)
    rows = boxes_state.shape[0]
    view = boxes_state.reshape(rows, N_WIDE, N_NARROW, N_WIDE, -1)
    boxes_state = jnp.transpose(view, (0, 3, 2, 1, 4)).reshape(rows, -1)
    boxes_state = rotate(product(switch_matrix, boxes_state), switch_angle, per_box)
    last_bit = N_NARROW.bit_length() - 2
    boxes_state = butterfly_level(boxes_state, level_self[1], level_peer[1], level_angle[1], last_bit, per_box)
    real_part = product(evaluate, boxes_state[:rank])
    imag_part = product(evaluate, boxes_state[rank:])
    cos_out = jnp.repeat(jnp.cos(out_angle), per_box, axis=1)
    sin_out = jnp.repeat(jnp.sin(out_angle), per_box, axis=1)
    return (cos_out * real_part - sin_out * imag_part).astype(jnp.bfloat16)
```

```python
import functools

import jax
import jax.numpy as jnp
from jax import lax
from jax.experimental import pallas as pl
from jax.experimental.pallas import tpu as pltpu
from jax.sharding import PartitionSpec as P

MESH = pl.DeviceIdType.MESH
F32 = jnp.float32
BF16 = jnp.bfloat16


def from_partner(value, axis, apart):
    mask = 2**apart
    pairs = [(source, source ^ mask) for source in range(lax.axis_size(axis))]
    return lax.ppermute(value, axis, pairs)


def product(left, right):
    return jnp.dot(left, right, precision=lax.Precision.HIGHEST, preferred_element_type=jnp.float32)


def rotate(boxes_state, phase_angle, per_box):
    rank = phase_angle.shape[0]
    cos_part = jnp.repeat(jnp.cos(phase_angle), per_box, axis=1)
    sin_part = jnp.repeat(jnp.sin(phase_angle), per_box, axis=1)
    real_part = boxes_state[:rank]
    imag_part = boxes_state[rank:]
    return jnp.concatenate(
        [cos_part * real_part - sin_part * imag_part, sin_part * real_part + cos_part * imag_part],
        axis=0,
    )


def butterfly_level(boxes_state, self_matrix, peer_matrix, phase_angle, bit, per_box):
    sent_state = boxes_state.astype(jnp.bfloat16)
    received = from_partner(sent_state, "narrow", bit)
    combined = product(self_matrix, boxes_state) + product(
        peer_matrix, received.astype(jnp.float32)
    )
    return rotate(combined, phase_angle, per_box)


def leaf_weights(lagrange, point_charges, point_angle, per_box):
    cos_leaf = jnp.repeat(jnp.cos(point_angle), per_box, axis=1)
    sin_leaf = jnp.repeat(jnp.sin(point_angle), per_box, axis=1)
    return jnp.concatenate(
        [product(lagrange, cos_leaf * point_charges), product(lagrange, sin_leaf * point_charges)],
        axis=0,
    )


def staged_body(
    charges,
    leaf_angle,
    lagrange,
    level_angle,
    level_self,
    level_peer,
    switch_angle,
    switch_matrix,
    out_angle,
    evaluate,
):
    per_box = charges.shape[1] // leaf_angle.shape[1]
    rank = lagrange.shape[0]
    last_bit = lax.axis_size("narrow").bit_length() - 2
    boxes_state = leaf_weights(lagrange, charges, leaf_angle, per_box)
    boxes_state = butterfly_level(
        boxes_state, level_self[0], level_peer[0], level_angle[0], 0, per_box
    )
    boxes_state = lax.all_to_all(boxes_state, "wide", split_axis=1, concat_axis=1, tiled=True)
    boxes_state = rotate(product(switch_matrix, boxes_state), switch_angle, per_box)
    boxes_state = butterfly_level(
        boxes_state, level_self[1], level_peer[1], level_angle[1], last_bit, per_box
    )
    real_part = product(evaluate, boxes_state[:rank])
    imag_part = product(evaluate, boxes_state[rank:])
    cos_out = jnp.repeat(jnp.cos(out_angle), per_box, axis=1)
    sin_out = jnp.repeat(jnp.sin(out_angle), per_box, axis=1)
    return (cos_out * real_part - sin_out * imag_part).astype(jnp.bfloat16)


def cos_sin(angle):
    half = angle * 0.5
    t = half * half
    s = half * (
        1.0
        + t * (-1 / 6 + t * (1 / 120 + t * (-1 / 5040 + t * (1 / 362880 + t * (-1 / 39916800)))))
    )
    c = 1.0 + t * (
        -1 / 2
        + t * (1 / 24 + t * (-1 / 720 + t * (1 / 40320 + t * (-1 / 3628800 + t / 479001600))))
    )
    return 1.0 - 2.0 * s * s, 2.0 * s * c


def split(value):
    high = value.astype(BF16)
    return high, (value - high.astype(F32)).astype(BF16)


def dot(left, right):
    return jnp.dot(left, right, preferred_element_type=F32)


def spread(boxes, columns, first, per_box):
    box = lax.broadcasted_iota(jnp.int32, (boxes, columns), 0)
    column = lax.broadcasted_iota(jnp.int32, (boxes, columns), 1) + first * per_box
    low = box * per_box
    once = jnp.where((column >= low) & (column < low + per_box), 1.0, 0.0).astype(BF16)
    return jnp.concatenate([once, once], axis=0)


def flip(index, bits):
    if bits == 0:
        return index
    if bits == 1:
        return index + 1 - 2 * lax.rem(index, 2)
    if bits == 2:
        return lax.rem(index + 2, 4)
    return 3 - index


def turn(real, imag, cos_part, sin_part):
    return cos_part * real - sin_part * imag, sin_part * real + cos_part * imag


def kernel(
    per_box,
    charges,
    leaf_angle,
    lagrange,
    level_angle,
    level_self,
    level_peer,
    switch_angle,
    switch_matrix,
    out_angle,
    evaluate,
    field,
    outbox,
    own,
    peer,
    peer_switch,
    cos_table,
    sin_table,
    cos_peer,
    sin_peer,
    wide_send,
    wide_recv,
    narrow_send,
    narrow_recv,
    switch_sems,
):
    me = lax.axis_index("wide")
    row = lax.axis_index("narrow")
    layer = me // 4
    place = lax.rem(me, 4)
    other = 1 - row
    rank, points = lagrange.shape
    angles = points + rank

    barrier = pltpu.get_barrier_semaphore()
    for bits in range(1, 16):
        to = flip(layer, bits // 4) * 4 + flip(place, bits % 4)
        pl.semaphore_signal(barrier, inc=1, device_id={"wide": to}, device_id_type=MESH)
    pl.semaphore_signal(barrier, inc=1, device_id={"narrow": other}, device_id_type=MESH)

    stacked = jnp.concatenate(
        [leaf_angle[...], level_angle[0], jnp.zeros((128 - angles, 128), F32)], axis=0
    )
    by_box = stacked.T
    high = by_box.astype(BF16).astype(F32)
    low = by_box - high
    for to in range(16):
        outbox[to, :points, :] = charges[:, to * 128 : (to + 1) * 128].astype(BF16)
        pair = jnp.concatenate([high[to * 8 : to * 8 + 8], low[to * 8 : to * 8 + 8]], axis=0)
        outbox[to, points : points + 16, :] = pair.astype(BF16)
    own[me] = outbox[me]

    def to_wide(bits):
        to = flip(layer, bits // 4) * 4 + flip(place, bits % 4)
        return pltpu.make_async_remote_copy(
            src_ref=outbox.at[to],
            dst_ref=own.at[me],
            send_sem=wide_send.at[to],
            recv_sem=wide_recv.at[me],
            device_id={"wide": to},
            device_id_type=MESH,
        )

    def from_wide(source):
        return pltpu.make_async_remote_copy(
            src_ref=outbox.at[source],
            dst_ref=own.at[source],
            send_sem=wide_send.at[source],
            recv_sem=wide_recv.at[source],
            device_id={"wide": source},
            device_id_type=MESH,
        )

    def across(source):
        return pltpu.make_async_remote_copy(
            src_ref=own.at[source],
            dst_ref=peer.at[source],
            send_sem=narrow_send.at[source],
            recv_sem=narrow_recv.at[source],
            device_id={"narrow": other},
            device_id_type=MESH,
        )

    switch_copy = pltpu.make_async_remote_copy(
        src_ref=switch_angle,
        dst_ref=peer_switch,
        send_sem=switch_sems.at[0],
        recv_sem=switch_sems.at[1],
        device_id={"narrow": other},
        device_id_type=MESH,
    )

    pl.semaphore_wait(barrier, 16)
    across(me).start()
    order = [1, 8, 12, 2, 9, 13, 3, 4, 10, 14, 5, 11, 15, 6, 7]
    for bits in order:
        to_wide(bits).start()
    switch_copy.start()

    def pass_on(group):
        for bits in range(4):
            if group or bits:
                source = flip(layer, group) * 4 + flip(place, bits)
                from_wide(source).wait_recv()
                across(source).start()

    group_columns = 4 * 128

    def fill(angle, first_row, cos_to, sin_to):
        rows = angle.shape[0]
        both = jnp.concatenate(cos_sin(angle), axis=0)
        halves = jnp.concatenate(split(both), axis=1)
        for group in range(4):
            columns = pl.ds(group * group_columns, group_columns)
            wide = dot(halves, spread(128, group_columns, group * group_columns // per_box, per_box))
            cos_to[pl.ds(first_row, rows), columns] = wide[:rows]
            sin_to[pl.ds(first_row, rows), columns] = wide[rows:]

    local = jnp.concatenate([switch_angle[...], level_angle[1], out_angle[...]], axis=0)
    fill(local, 0, cos_table, sin_table)

    lag_high, lag_low = split(lagrange[...])
    leaf_matrix = jnp.concatenate([lag_high, lag_low, lag_high], axis=1)
    eva_high, eva_low = split(evaluate[...])
    out_matrix = jnp.concatenate([eva_high, eva_low, eva_high], axis=1)
    both_high, both_low = split(
        jnp.concatenate(
            [
                jnp.concatenate([level_self[0], level_peer[0]], axis=1),
                jnp.concatenate([level_peer[0], level_self[0]], axis=1),
            ],
            axis=0,
        )
    )
    swi_high, swi_low = split(switch_matrix[...])
    swi_matrix = jnp.concatenate([swi_high, swi_low], axis=1)
    last_high, last_low = split(jnp.concatenate([level_self[1], level_peer[1]], axis=1))
    repeat = spread(32, group_columns, 0, per_box)

    def leaf(box, base):
        charge = jnp.concatenate([box[base + i, :points, :] for i in range(4)], axis=1).astype(F32)
        parts = [box[base + i, points : points + 16, :].astype(F32) for i in range(4)]
        angle = jnp.concatenate([part[:8] + part[8:] for part in parts], axis=0)
        both = jnp.concatenate(cos_sin(angle), axis=1)
        halves = jnp.concatenate(split(both), axis=0)
        wide = lax.dot_general(
            halves, repeat, (((0,), (0,)), ((), ())), preferred_element_type=F32
        )
        cos_part, sin_part = wide[:128], wide[128:]
        weighted = jnp.concatenate([cos_part[:points] * charge, sin_part[:points] * charge], axis=1)
        high, low = split(weighted)
        state = dot(leaf_matrix, jnp.concatenate([high, high, low], axis=0))
        turned = cos_part[points:angles], sin_part[points:angles]
        return [state[:, :group_columns], state[:, group_columns:]], turned

    def compute(group):
        where = flip(layer, group)
        for bits in range(4):
            across(where * 4 + bits).wait_recv()
        columns = pl.ds(pl.multiple_of(where * group_columns, group_columns), group_columns)
        state_own, turn_own = leaf(own, where * 4)
        state_peer, turn_peer = leaf(peer, where * 4)
        state = jnp.concatenate(state_own + state_peer, axis=0).astype(BF16)
        first = dot(both_high, state) + dot(both_low, state)
        own_real, own_imag = turn(first[:rank], first[rank : 2 * rank], *turn_own)
        peer_real, peer_imag = turn(first[2 * rank : 3 * rank], first[3 * rank :], *turn_peer)
        moved = jnp.concatenate(
            [
                jnp.concatenate([own_real, peer_real], axis=1),
                jnp.concatenate([own_imag, peer_imag], axis=1),
            ],
            axis=0,
        ).astype(BF16)
        middle = dot(swi_matrix, jnp.concatenate([moved, moved], axis=0))
        own_real, own_imag = turn(
            middle[:rank, :group_columns],
            middle[rank:, :group_columns],
            cos_table[:rank, columns],
            sin_table[:rank, columns],
        )
        peer_real, peer_imag = turn(
            middle[:rank, group_columns:],
            middle[rank:, group_columns:],
            cos_peer[:, columns],
            sin_peer[:, columns],
        )
        state = jnp.concatenate([own_real, own_imag, peer_real, peer_imag], axis=0).astype(BF16)
        last = dot(last_high, state) + dot(last_low, state)
        real, imag = turn(
            last[:rank],
            last[rank:],
            cos_table[rank : 2 * rank, columns],
            sin_table[rank : 2 * rank, columns],
        )
        high, low = split(jnp.concatenate([real, imag], axis=1))
        value = dot(out_matrix, jnp.concatenate([high, high, low], axis=0))
        field[:, columns] = (
            cos_table[2 * rank :, columns] * value[:, :group_columns]
            - sin_table[2 * rank :, columns] * value[:, group_columns:]
        ).astype(BF16)

    pass_on(0)
    pass_on(1)
    switch_copy.wait_recv()
    fill(peer_switch[...], 0, cos_peer, sin_peer)
    compute(0)
    pass_on(2)
    compute(1)
    pass_on(3)
    compute(2)
    compute(3)

    for bits in range(1, 16):
        to_wide(bits).wait_send()
    for source in range(16):
        across(source).wait_send()
    switch_copy.wait_send()


def paired_body(*operands):
    charges, leaf_angle, lagrange = operands[:3]
    points, columns = charges.shape
    rank = lagrange.shape[0]
    per_box = columns // leaf_angle.shape[1]
    return pl.pallas_call(
        functools.partial(kernel, per_box),
        out_shape=jax.ShapeDtypeStruct((points, columns), BF16),
        in_specs=[pl.BlockSpec(memory_space=pltpu.VMEM)] * len(operands),
        out_specs=pl.BlockSpec(memory_space=pltpu.VMEM),
        scratch_shapes=[
            pltpu.VMEM((16, points + 16, 128), BF16),
            pltpu.VMEM((16, points + 16, 128), BF16),
            pltpu.VMEM((16, points + 16, 128), BF16),
            pltpu.VMEM((rank, 128), F32),
            pltpu.VMEM((2 * rank + points, columns), F32),
            pltpu.VMEM((2 * rank + points, columns), F32),
            pltpu.VMEM((rank, columns), F32),
            pltpu.VMEM((rank, columns), F32),
            pltpu.SemaphoreType.DMA((16,)),
            pltpu.SemaphoreType.DMA((16,)),
            pltpu.SemaphoreType.DMA((16,)),
            pltpu.SemaphoreType.DMA((16,)),
            pltpu.SemaphoreType.DMA((2,)),
        ],
        compiler_params=pltpu.CompilerParams(
            collective_id=0, has_side_effects=True, vmem_limit_bytes=40 * 1024 * 1024
        ),
        cost_estimate=pl.CostEstimate(
            flops=2 * 60000 * 2 * columns, bytes_accessed=4 * points * columns, transcendentals=0
        ),
    )(*operands)


def fits_pairs(mesh, charges, leaf_angle, lagrange):
    devices = mesh.shape["wide"] * mesh.shape["narrow"]
    columns = charges.shape[1] // devices
    boxes = leaf_angle.shape[1] // devices
    return (
        mesh.shape["narrow"] == 2
        and mesh.shape["wide"] == 16
        and columns == 2048
        and boxes == 128
        and charges.shape[0] % 16 == 0
        and lagrange.shape[0] % 16 == 0
        and charges.shape[0] + lagrange.shape[0] <= 128
    )


def solution(mesh):
    def program(charges, leaf_angle, lagrange, *rest):
        fits = fits_pairs(mesh, charges, leaf_angle, lagrange)
        return jax.shard_map(
            paired_body if fits else staged_body,
            mesh=mesh,
            in_specs=(
                P(None, ("wide", "narrow")),
                P(None, ("wide", "narrow")),
                P(),
                P(None, None, ("wide", "narrow")),
                P(),
                P(),
                P(None, ("wide", "narrow")),
                P(),
                P(None, ("wide", "narrow")),
                P(),
            ),
            out_specs=P(None, ("wide", "narrow")),
            check_vma=False,
        )(charges, leaf_angle, lagrange, *rest)

    return program
```

```python
import functools

import jax
import jax.numpy as jnp
from jax import lax
from jax.experimental import pallas as pl
from jax.experimental.pallas import tpu as pltpu
from jax.sharding import PartitionSpec as P

MESH = pl.DeviceIdType.MESH
F32 = jnp.float32
BF16 = jnp.bfloat16


def from_partner(value, axis, apart):
    mask = 2**apart
    pairs = [(source, source ^ mask) for source in range(lax.axis_size(axis))]
    return lax.ppermute(value, axis, pairs)


def product(left, right):
    return jnp.dot(left, right, precision=lax.Precision.HIGHEST, preferred_element_type=jnp.float32)


def rotate(boxes_state, phase_angle, per_box):
    rank = phase_angle.shape[0]
    cos_part = jnp.repeat(jnp.cos(phase_angle), per_box, axis=1)
    sin_part = jnp.repeat(jnp.sin(phase_angle), per_box, axis=1)
    real_part = boxes_state[:rank]
    imag_part = boxes_state[rank:]
    return jnp.concatenate(
        [cos_part * real_part - sin_part * imag_part, sin_part * real_part + cos_part * imag_part],
        axis=0,
    )


def butterfly_level(boxes_state, self_matrix, peer_matrix, phase_angle, bit, per_box):
    sent_state = boxes_state.astype(jnp.bfloat16)
    received = from_partner(sent_state, "narrow", bit)
    combined = product(self_matrix, boxes_state) + product(
        peer_matrix, received.astype(jnp.float32)
    )
    return rotate(combined, phase_angle, per_box)


def leaf_weights(lagrange, point_charges, point_angle, per_box):
    cos_leaf = jnp.repeat(jnp.cos(point_angle), per_box, axis=1)
    sin_leaf = jnp.repeat(jnp.sin(point_angle), per_box, axis=1)
    return jnp.concatenate(
        [product(lagrange, cos_leaf * point_charges), product(lagrange, sin_leaf * point_charges)],
        axis=0,
    )


def staged_body(
    charges,
    leaf_angle,
    lagrange,
    level_angle,
    level_self,
    level_peer,
    switch_angle,
    switch_matrix,
    out_angle,
    evaluate,
):
    per_box = charges.shape[1] // leaf_angle.shape[1]
    rank = lagrange.shape[0]
    last_bit = lax.axis_size("narrow").bit_length() - 2
    boxes_state = leaf_weights(lagrange, charges, leaf_angle, per_box)
    boxes_state = butterfly_level(
        boxes_state, level_self[0], level_peer[0], level_angle[0], 0, per_box
    )
    boxes_state = lax.all_to_all(boxes_state, "wide", split_axis=1, concat_axis=1, tiled=True)
    boxes_state = rotate(product(switch_matrix, boxes_state), switch_angle, per_box)
    boxes_state = butterfly_level(
        boxes_state, level_self[1], level_peer[1], level_angle[1], last_bit, per_box
    )
    real_part = product(evaluate, boxes_state[:rank])
    imag_part = product(evaluate, boxes_state[rank:])
    cos_out = jnp.repeat(jnp.cos(out_angle), per_box, axis=1)
    sin_out = jnp.repeat(jnp.sin(out_angle), per_box, axis=1)
    return (cos_out * real_part - sin_out * imag_part).astype(jnp.bfloat16)


def cos_sin(angle):
    half = angle * 0.5
    t = half * half
    s = half * (
        1.0
        + t * (-1 / 6 + t * (1 / 120 + t * (-1 / 5040 + t * (1 / 362880 + t * (-1 / 39916800)))))
    )
    c = 1.0 + t * (
        -1 / 2
        + t * (1 / 24 + t * (-1 / 720 + t * (1 / 40320 + t * (-1 / 3628800 + t / 479001600))))
    )
    return 1.0 - 2.0 * s * s, 2.0 * s * c


def split(value):
    high = value.astype(BF16)
    return high, (value - high.astype(F32)).astype(BF16)


def dot(left, right):
    return jnp.dot(left, right, preferred_element_type=F32)


def spread(boxes, columns, first, per_box):
    box = lax.broadcasted_iota(jnp.int32, (boxes, columns), 0)
    column = lax.broadcasted_iota(jnp.int32, (boxes, columns), 1) + first * per_box
    low = box * per_box
    once = jnp.where((column >= low) & (column < low + per_box), 1.0, 0.0).astype(BF16)
    return jnp.concatenate([once, once], axis=0)


def flip(index, bits):
    if bits == 0:
        return index
    if bits == 1:
        return index + 1 - 2 * lax.rem(index, 2)
    if bits == 2:
        return lax.rem(index + 2, 4)
    return 3 - index


def turn(real, imag, cos_part, sin_part):
    return cos_part * real - sin_part * imag, sin_part * real + cos_part * imag


def kernel(
    per_box,
    *refs,
):
    given, refs = refs[:10], refs[10:]
    field, (held, refs) = refs[0], (refs[1:11], refs[11:])
    (
        charges,
        leaf_angle,
        lagrange,
        level_angle,
        level_self,
        level_peer,
        switch_angle,
        switch_matrix,
        out_angle,
        evaluate,
    ) = held
    (
    outbox,
    own,
    peer,
    peer_switch,
    cos_table,
    sin_table,
    cos_peer,
    sin_peer,
    wide_send,
    wide_recv,
    narrow_send,
    narrow_recv,
    switch_sems,
    load_sems,
    ) = refs
    loads = [pltpu.make_async_copy(g, h, load_sems.at[i]) for i, (g, h) in enumerate(zip(given, held))]
    first_loads = [1, 3, 0, 6]
    later_loads = [i for i in range(10) if i not in first_loads]
    for i in first_loads + later_loads:
        loads[i].start()
    me = lax.axis_index("wide")
    row = lax.axis_index("narrow")
    layer = me // 4
    place = lax.rem(me, 4)
    other = 1 - row
    rank, points = lagrange.shape
    angles = points + rank

    barrier = pltpu.get_barrier_semaphore()
    for bits in range(1, 16):
        to = flip(layer, bits // 4) * 4 + flip(place, bits % 4)
        pl.semaphore_signal(barrier, inc=1, device_id={"wide": to}, device_id_type=MESH)
    pl.semaphore_signal(barrier, inc=1, device_id={"narrow": other}, device_id_type=MESH)

    for i in first_loads:
        loads[i].wait()

    stacked = jnp.concatenate(
        [leaf_angle[...], level_angle[0], jnp.zeros((128 - angles, 128), F32)], axis=0
    )
    by_box = stacked.T
    high = by_box.astype(BF16).astype(F32)
    low = by_box - high
    for to in range(16):
        outbox[to, :points, :] = charges[:, to * 128 : (to + 1) * 128].astype(BF16)
        pair = jnp.concatenate([high[to * 8 : to * 8 + 8], low[to * 8 : to * 8 + 8]], axis=0)
        outbox[to, points : points + 16, :] = pair.astype(BF16)
    own[me] = outbox[me]

    def to_wide(bits):
        to = flip(layer, bits // 4) * 4 + flip(place, bits % 4)
        return pltpu.make_async_remote_copy(
            src_ref=outbox.at[to],
            dst_ref=own.at[me],
            send_sem=wide_send.at[to],
            recv_sem=wide_recv.at[me],
            device_id={"wide": to},
            device_id_type=MESH,
        )

    def from_wide(source):
        return pltpu.make_async_remote_copy(
            src_ref=outbox.at[source],
            dst_ref=own.at[source],
            send_sem=wide_send.at[source],
            recv_sem=wide_recv.at[source],
            device_id={"wide": source},
            device_id_type=MESH,
        )

    def across(source):
        return pltpu.make_async_remote_copy(
            src_ref=own.at[source],
            dst_ref=peer.at[source],
            send_sem=narrow_send.at[source],
            recv_sem=narrow_recv.at[source],
            device_id={"narrow": other},
            device_id_type=MESH,
        )

    switch_copy = pltpu.make_async_remote_copy(
        src_ref=switch_angle,
        dst_ref=peer_switch,
        send_sem=switch_sems.at[0],
        recv_sem=switch_sems.at[1],
        device_id={"narrow": other},
        device_id_type=MESH,
    )

    pl.semaphore_wait(barrier, 16)
    across(me).start()
    order = [1, 8, 12, 2, 9, 13, 3, 4, 10, 14, 5, 11, 15, 6, 7]
    for bits in order:
        to_wide(bits).start()
    switch_copy.start()

    def pass_on(group):
        for bits in range(4):
            if group or bits:
                source = flip(layer, group) * 4 + flip(place, bits)
                from_wide(source).wait_recv()
                across(source).start()

    for i in later_loads:
        loads[i].wait()

    group_columns = 4 * 128

    def fill(angle, first_row, cos_to, sin_to):
        rows = angle.shape[0]
        both = jnp.concatenate(cos_sin(angle), axis=0)
        halves = jnp.concatenate(split(both), axis=1)
        for group in range(4):
            columns = pl.ds(group * group_columns, group_columns)
            wide = dot(halves, spread(128, group_columns, group * group_columns // per_box, per_box))
            cos_to[pl.ds(first_row, rows), columns] = wide[:rows]
            sin_to[pl.ds(first_row, rows), columns] = wide[rows:]

    local = jnp.concatenate([switch_angle[...], level_angle[1], out_angle[...]], axis=0)
    fill(local, 0, cos_table, sin_table)

    lag_high, lag_low = split(lagrange[...])
    leaf_matrix = jnp.concatenate([lag_high, lag_low, lag_high], axis=1)
    eva_high, eva_low = split(evaluate[...].T)
    out_matrix = jnp.concatenate([eva_high, eva_low, eva_high], axis=1)
    both_matrix = split(
        jnp.concatenate(
            [
                jnp.concatenate([level_self[0], level_peer[0]], axis=1),
                jnp.concatenate([level_peer[0], level_self[0]], axis=1),
            ],
            axis=0,
        )
    )
    both_matrix = jnp.concatenate(both_matrix, axis=0)
    swi_high, swi_low = split(switch_matrix[...])
    swi_matrix = jnp.concatenate([swi_high, swi_low], axis=1)
    last_matrix = split(jnp.concatenate([level_self[1], level_peer[1]], axis=1))
    last_matrix = jnp.concatenate(last_matrix, axis=0)
    repeat = spread(32, group_columns, 0, per_box)

    def leaf(box, base):
        charge = jnp.concatenate([box[base + i, :points, :] for i in range(4)], axis=1).astype(F32)
        parts = [box[base + i, points : points + 16, :].astype(F32) for i in range(4)]
        angle = jnp.concatenate([part[:8] + part[8:] for part in parts], axis=0)
        both = jnp.concatenate(cos_sin(angle), axis=1)
        halves = jnp.concatenate(split(both), axis=0)
        wide = lax.dot_general(
            halves, repeat, (((0,), (0,)), ((), ())), preferred_element_type=F32
        )
        cos_part, sin_part = wide[:128], wide[128:]
        weighted = jnp.concatenate([cos_part[:points] * charge, sin_part[:points] * charge], axis=1)
        high, low = split(weighted)
        state = dot(leaf_matrix, jnp.concatenate([high, high, low], axis=0))
        turned = cos_part[points:angles], sin_part[points:angles]
        return [state[:, :group_columns], state[:, group_columns:]], turned

    def compute(group):
        where = flip(layer, group)
        columns = pl.ds(pl.multiple_of(where * group_columns, group_columns), group_columns)
        state_own, turn_own = leaf(own, where * 4)
        for bits in range(4):
            across(where * 4 + bits).wait_recv()
        state_peer, turn_peer = leaf(peer, where * 4)
        state = jnp.concatenate(state_own + state_peer, axis=0).astype(BF16)
        first = dot(both_matrix, state)
        first = first[: 4 * rank] + first[4 * rank :]
        own_real, own_imag = turn(first[:rank], first[rank : 2 * rank], *turn_own)
        peer_real, peer_imag = turn(first[2 * rank : 3 * rank], first[3 * rank :], *turn_peer)
        moved = jnp.concatenate(
            [
                jnp.concatenate([own_real, peer_real], axis=1),
                jnp.concatenate([own_imag, peer_imag], axis=1),
            ],
            axis=0,
        ).astype(BF16)
        middle = dot(swi_matrix, jnp.concatenate([moved, moved], axis=0))
        own_real, own_imag = turn(
            middle[:rank, :group_columns],
            middle[rank:, :group_columns],
            cos_table[:rank, columns],
            sin_table[:rank, columns],
        )
        peer_real, peer_imag = turn(
            middle[:rank, group_columns:],
            middle[rank:, group_columns:],
            cos_peer[:, columns],
            sin_peer[:, columns],
        )
        state = jnp.concatenate([own_real, own_imag, peer_real, peer_imag], axis=0).astype(BF16)
        last = dot(last_matrix, state)
        last = last[: 2 * rank] + last[2 * rank :]
        real, imag = turn(
            last[:rank],
            last[rank:],
            cos_table[rank : 2 * rank, columns],
            sin_table[rank : 2 * rank, columns],
        )
        high, low = split(jnp.concatenate([real, imag], axis=1))
        value = dot(out_matrix, jnp.concatenate([high, high, low], axis=0))
        field[:, columns] = (
            cos_table[2 * rank :, columns] * value[:, :group_columns]
            - sin_table[2 * rank :, columns] * value[:, group_columns:]
        ).astype(BF16)

    pass_on(0)
    pass_on(1)
    switch_copy.wait_recv()
    fill(peer_switch[...], 0, cos_peer, sin_peer)
    compute(0)
    pass_on(2)
    compute(1)
    pass_on(3)
    compute(2)
    compute(3)

    for bits in range(1, 16):
        to_wide(bits).wait_send()
    for source in range(16):
        across(source).wait_send()
    switch_copy.wait_send()


def paired_body(*operands):
    charges, leaf_angle, lagrange = operands[:3]
    points, columns = charges.shape
    rank = lagrange.shape[0]
    per_box = columns // leaf_angle.shape[1]
    operands = operands[:-1] + (operands[-1].T,)
    return pl.pallas_call(
        functools.partial(kernel, per_box),
        out_shape=jax.ShapeDtypeStruct((points, columns), BF16),
        in_specs=[pl.BlockSpec(memory_space=pltpu.HBM)] * len(operands),
        out_specs=pl.BlockSpec(memory_space=pltpu.VMEM),
        scratch_shapes=[pltpu.VMEM(operand.shape, F32) for operand in operands]
        + [
            pltpu.VMEM((16, points + 16, 128), BF16),
            pltpu.VMEM((16, points + 16, 128), BF16),
            pltpu.VMEM((16, points + 16, 128), BF16),
            pltpu.VMEM((rank, 128), F32),
            pltpu.VMEM((2 * rank + points, columns), F32),
            pltpu.VMEM((2 * rank + points, columns), F32),
            pltpu.VMEM((rank, columns), F32),
            pltpu.VMEM((rank, columns), F32),
            pltpu.SemaphoreType.DMA((16,)),
            pltpu.SemaphoreType.DMA((16,)),
            pltpu.SemaphoreType.DMA((16,)),
            pltpu.SemaphoreType.DMA((16,)),
            pltpu.SemaphoreType.DMA((2,)),
            pltpu.SemaphoreType.DMA((len(operands),)),
        ],
        compiler_params=pltpu.CompilerParams(
            collective_id=0, has_side_effects=True, vmem_limit_bytes=60 * 1024 * 1024
        ),
        cost_estimate=pl.CostEstimate(
            flops=2 * 60000 * 2 * columns, bytes_accessed=4 * points * columns, transcendentals=0
        ),
    )(*operands)


def fits_pairs(mesh, charges, leaf_angle, lagrange):
    devices = mesh.shape["wide"] * mesh.shape["narrow"]
    columns = charges.shape[1] // devices
    boxes = leaf_angle.shape[1] // devices
    return (
        mesh.shape["narrow"] == 2
        and mesh.shape["wide"] == 16
        and columns == 2048
        and boxes == 128
        and charges.shape[0] % 16 == 0
        and lagrange.shape[0] % 16 == 0
        and charges.shape[0] + lagrange.shape[0] <= 128
    )


def solution(mesh):
    def program(charges, leaf_angle, lagrange, *rest):
        fits = fits_pairs(mesh, charges, leaf_angle, lagrange)
        return jax.shard_map(
            paired_body if fits else staged_body,
            mesh=mesh,
            in_specs=(
                P(None, ("wide", "narrow")),
                P(None, ("wide", "narrow")),
                P(),
                P(None, None, ("wide", "narrow")),
                P(),
                P(),
                P(None, ("wide", "narrow")),
                P(),
                P(None, ("wide", "narrow")),
                P(),
            ),
            out_specs=P(None, ("wide", "narrow")),
            check_vma=False,
        )(charges, leaf_angle, lagrange, *rest)

    return program
```

```python
import functools

import jax
import jax.numpy as jnp
from jax import lax
from jax.experimental import pallas as pl
from jax.experimental.pallas import tpu as pltpu
from jax.sharding import PartitionSpec as P

MESH = pl.DeviceIdType.MESH
F32 = jnp.float32
BF16 = jnp.bfloat16


def from_partner(value, axis, apart):
    mask = 2**apart
    pairs = [(source, source ^ mask) for source in range(lax.axis_size(axis))]
    return lax.ppermute(value, axis, pairs)


def product(left, right):
    return jnp.dot(left, right, precision=lax.Precision.HIGHEST, preferred_element_type=jnp.float32)


def rotate(boxes_state, phase_angle, per_box):
    rank = phase_angle.shape[0]
    cos_part = jnp.repeat(jnp.cos(phase_angle), per_box, axis=1)
    sin_part = jnp.repeat(jnp.sin(phase_angle), per_box, axis=1)
    real_part = boxes_state[:rank]
    imag_part = boxes_state[rank:]
    return jnp.concatenate(
        [cos_part * real_part - sin_part * imag_part, sin_part * real_part + cos_part * imag_part],
        axis=0,
    )


def butterfly_level(boxes_state, self_matrix, peer_matrix, phase_angle, bit, per_box):
    sent_state = boxes_state.astype(jnp.bfloat16)
    received = from_partner(sent_state, "narrow", bit)
    combined = product(self_matrix, boxes_state) + product(
        peer_matrix, received.astype(jnp.float32)
    )
    return rotate(combined, phase_angle, per_box)


def leaf_weights(lagrange, point_charges, point_angle, per_box):
    cos_leaf = jnp.repeat(jnp.cos(point_angle), per_box, axis=1)
    sin_leaf = jnp.repeat(jnp.sin(point_angle), per_box, axis=1)
    return jnp.concatenate(
        [product(lagrange, cos_leaf * point_charges), product(lagrange, sin_leaf * point_charges)],
        axis=0,
    )


def staged_body(
    charges,
    leaf_angle,
    lagrange,
    level_angle,
    level_self,
    level_peer,
    switch_angle,
    switch_matrix,
    out_angle,
    evaluate,
):
    per_box = charges.shape[1] // leaf_angle.shape[1]
    rank = lagrange.shape[0]
    last_bit = lax.axis_size("narrow").bit_length() - 2
    boxes_state = leaf_weights(lagrange, charges, leaf_angle, per_box)
    boxes_state = butterfly_level(
        boxes_state, level_self[0], level_peer[0], level_angle[0], 0, per_box
    )
    boxes_state = lax.all_to_all(boxes_state, "wide", split_axis=1, concat_axis=1, tiled=True)
    boxes_state = rotate(product(switch_matrix, boxes_state), switch_angle, per_box)
    boxes_state = butterfly_level(
        boxes_state, level_self[1], level_peer[1], level_angle[1], last_bit, per_box
    )
    real_part = product(evaluate, boxes_state[:rank])
    imag_part = product(evaluate, boxes_state[rank:])
    cos_out = jnp.repeat(jnp.cos(out_angle), per_box, axis=1)
    sin_out = jnp.repeat(jnp.sin(out_angle), per_box, axis=1)
    return (cos_out * real_part - sin_out * imag_part).astype(jnp.bfloat16)


def cos_sin(angle):
    half = angle * 0.5
    t = half * half
    s = half * (
        1.0
        + t * (-1 / 6 + t * (1 / 120 + t * (-1 / 5040 + t * (1 / 362880 + t * (-1 / 39916800)))))
    )
    c = 1.0 + t * (
        -1 / 2
        + t * (1 / 24 + t * (-1 / 720 + t * (1 / 40320 + t * (-1 / 3628800 + t / 479001600))))
    )
    return 1.0 - 2.0 * s * s, 2.0 * s * c


def split(value):
    high = value.astype(BF16)
    return high, (value - high.astype(F32)).astype(BF16)


def dot(left, right):
    return jnp.dot(left, right, preferred_element_type=F32)


def spread(boxes, columns, first, per_box):
    box = lax.broadcasted_iota(jnp.int32, (boxes, columns), 0)
    column = lax.broadcasted_iota(jnp.int32, (boxes, columns), 1) + first * per_box
    low = box * per_box
    once = jnp.where((column >= low) & (column < low + per_box), 1.0, 0.0).astype(BF16)
    return jnp.concatenate([once, once], axis=0)


def flip(index, bits):
    if bits == 0:
        return index
    if bits == 1:
        return index + 1 - 2 * lax.rem(index, 2)
    if bits == 2:
        return lax.rem(index + 2, 4)
    return 3 - index


def turn(real, imag, cos_part, sin_part):
    return cos_part * real - sin_part * imag, sin_part * real + cos_part * imag


def kernel(
    per_box,
    *refs,
):
    given, refs = refs[:10], refs[10:]
    field, (held, refs) = refs[0], (refs[1:11], refs[11:])
    (
        charges,
        leaf_angle,
        lagrange,
        level_angle,
        level_self,
        level_peer,
        switch_angle,
        switch_matrix,
        out_angle,
        evaluate,
    ) = held
    (
    outbox,
    own,
    peer,
    peer_switch,
    cos_table,
    sin_table,
    cos_peer,
    sin_peer,
    wide_send,
    wide_recv,
    narrow_send,
    narrow_recv,
    switch_sems,
    load_sems,
    ) = refs
    loads = [pltpu.make_async_copy(g, h, load_sems.at[i]) for i, (g, h) in enumerate(zip(given, held))]
    first_loads = [1, 3, 0, 6]
    later_loads = [i for i in range(10) if i not in first_loads]
    for i in first_loads + later_loads:
        loads[i].start()
    me = lax.axis_index("wide")
    row = lax.axis_index("narrow")
    layer = me // 4
    place = lax.rem(me, 4)
    other = 1 - row
    rank, points = lagrange.shape
    angles = points + rank

    barrier = pltpu.get_barrier_semaphore()
    for bits in range(1, 16):
        to = flip(layer, bits // 4) * 4 + flip(place, bits % 4)
        pl.semaphore_signal(barrier, inc=1, device_id={"wide": to}, device_id_type=MESH)
    pl.semaphore_signal(barrier, inc=1, device_id={"narrow": other}, device_id_type=MESH)

    for i in first_loads:
        loads[i].wait()

    stacked = jnp.concatenate(
        [leaf_angle[...], level_angle[0], jnp.zeros((128 - angles, 128), F32)], axis=0
    )
    by_box = stacked.T
    high = by_box.astype(BF16).astype(F32)
    low = by_box - high
    for to in range(16):
        outbox[to, :points, :] = charges[:, to * 128 : (to + 1) * 128].astype(BF16)
        pair = jnp.concatenate([high[to * 8 : to * 8 + 8], low[to * 8 : to * 8 + 8]], axis=0)
        outbox[to, points : points + 16, :] = pair.astype(BF16)
    own[me] = outbox[me]

    def to_wide(bits):
        to = flip(layer, bits // 4) * 4 + flip(place, bits % 4)
        return pltpu.make_async_remote_copy(
            src_ref=outbox.at[to],
            dst_ref=own.at[me],
            send_sem=wide_send.at[to],
            recv_sem=wide_recv.at[me],
            device_id={"wide": to},
            device_id_type=MESH,
        )

    def from_wide(source):
        return pltpu.make_async_remote_copy(
            src_ref=outbox.at[source],
            dst_ref=own.at[source],
            send_sem=wide_send.at[source],
            recv_sem=wide_recv.at[source],
            device_id={"wide": source},
            device_id_type=MESH,
        )

    def across(source):
        return pltpu.make_async_remote_copy(
            src_ref=own.at[source],
            dst_ref=peer.at[source],
            send_sem=narrow_send.at[source],
            recv_sem=narrow_recv.at[source],
            device_id={"narrow": other},
            device_id_type=MESH,
        )

    switch_copy = pltpu.make_async_remote_copy(
        src_ref=switch_angle,
        dst_ref=peer_switch,
        send_sem=switch_sems.at[0],
        recv_sem=switch_sems.at[1],
        device_id={"narrow": other},
        device_id_type=MESH,
    )

    pl.semaphore_wait(barrier, 16)
    across(me).start()
    order = [1, 8, 12, 2, 9, 13, 3, 4, 10, 14, 5, 11, 15, 6, 7]
    for bits in order:
        to_wide(bits).start()
    switch_copy.start()

    def pass_on(group, half):
        for bits in (2 * half, 2 * half + 1):
            if group or bits:
                source = flip(layer, group) * 4 + flip(place, bits)
                from_wide(source).wait_recv()
                across(source).start()

    for i in later_loads:
        loads[i].wait()

    fill_columns = 4 * 128
    group_columns = 2 * 128

    def fill(angle, first_row, cos_to, sin_to):
        rows = angle.shape[0]
        both = jnp.concatenate(cos_sin(angle), axis=0)
        halves = jnp.concatenate(split(both), axis=1)
        for group in range(4):
            columns = pl.ds(group * fill_columns, fill_columns)
            wide = dot(halves, spread(128, fill_columns, group * fill_columns // per_box, per_box))
            cos_to[pl.ds(first_row, rows), columns] = wide[:rows]
            sin_to[pl.ds(first_row, rows), columns] = wide[rows:]

    local = jnp.concatenate([switch_angle[...], level_angle[1], out_angle[...]], axis=0)
    fill(local, 0, cos_table, sin_table)

    lag_high, lag_low = split(lagrange[...])
    leaf_matrix = jnp.concatenate([lag_high, lag_low], axis=1)
    eva_high, eva_low = split(evaluate[...].T)
    out_matrix = jnp.concatenate([eva_high, eva_low, eva_high], axis=1)
    both_matrix = split(
        jnp.concatenate(
            [
                jnp.concatenate([level_self[0], level_peer[0]], axis=1),
                jnp.concatenate([level_peer[0], level_self[0]], axis=1),
            ],
            axis=0,
        )
    )
    both_matrix = jnp.concatenate(both_matrix, axis=0)
    swi_high, swi_low = split(switch_matrix[...])
    swi_matrix = jnp.concatenate([swi_high, swi_low], axis=1)
    last_matrix = split(jnp.concatenate([level_self[1], level_peer[1]], axis=1))
    last_matrix = jnp.concatenate(last_matrix, axis=0)
    repeat = spread(16, group_columns, 0, per_box)

    def leaf(box, base):
        charge = jnp.concatenate([box[base + i, :points, :] for i in range(2)], axis=1).astype(F32)
        parts = [box[base + i, points : points + 16, :].astype(F32) for i in range(2)]
        angle = jnp.concatenate([part[:8] + part[8:] for part in parts], axis=0)
        both = jnp.concatenate(cos_sin(angle), axis=1)
        halves = jnp.concatenate(split(both), axis=0)
        wide = lax.dot_general(
            halves, repeat, (((0,), (0,)), ((), ())), preferred_element_type=F32
        )
        cos_part, sin_part = wide[:128], wide[128:]
        weighted = jnp.concatenate([cos_part[:points] * charge, sin_part[:points] * charge], axis=1)
        weighted = weighted.astype(BF16)
        state = dot(leaf_matrix, jnp.concatenate([weighted, weighted], axis=0))
        turned = cos_part[points:angles], sin_part[points:angles]
        return [state[:, :group_columns], state[:, group_columns:]], turned

    def compute(group, half):
        base = flip(layer, group) * 4 + flip(place // 2, half) * 2
        columns = pl.ds(pl.multiple_of(base * 128, group_columns), group_columns)
        state_own, turn_own = leaf(own, base)
        for i in range(2):
            across(base + i).wait_recv()
        state_peer, turn_peer = leaf(peer, base)
        state = jnp.concatenate(state_own + state_peer, axis=0).astype(BF16)
        first = dot(both_matrix, state)
        first = first[: 4 * rank] + first[4 * rank :]
        own_real, own_imag = turn(first[:rank], first[rank : 2 * rank], *turn_own)
        peer_real, peer_imag = turn(first[2 * rank : 3 * rank], first[3 * rank :], *turn_peer)
        moved = jnp.concatenate(
            [
                jnp.concatenate([own_real, peer_real], axis=1),
                jnp.concatenate([own_imag, peer_imag], axis=1),
            ],
            axis=0,
        ).astype(BF16)
        middle = dot(swi_matrix, jnp.concatenate([moved, moved], axis=0))
        own_real, own_imag = turn(
            middle[:rank, :group_columns],
            middle[rank:, :group_columns],
            cos_table[:rank, columns],
            sin_table[:rank, columns],
        )
        peer_real, peer_imag = turn(
            middle[:rank, group_columns:],
            middle[rank:, group_columns:],
            cos_peer[:, columns],
            sin_peer[:, columns],
        )
        state = jnp.concatenate([own_real, own_imag, peer_real, peer_imag], axis=0).astype(BF16)
        last = dot(last_matrix, state)
        last = last[: 2 * rank] + last[2 * rank :]
        real, imag = turn(
            last[:rank],
            last[rank:],
            cos_table[rank : 2 * rank, columns],
            sin_table[rank : 2 * rank, columns],
        )
        high, low = split(jnp.concatenate([real, imag], axis=1))
        value = dot(out_matrix, jnp.concatenate([high, high, low], axis=0))
        field[:, columns] = (
            cos_table[2 * rank :, columns] * value[:, :group_columns]
            - sin_table[2 * rank :, columns] * value[:, group_columns:]
        ).astype(BF16)

    pass_on(0, 0)
    pass_on(0, 1)
    pass_on(1, 0)
    pass_on(1, 1)
    switch_copy.wait_recv()
    fill(peer_switch[...], 0, cos_peer, sin_peer)
    compute(0, 0)
    pass_on(2, 0)
    compute(0, 1)
    pass_on(3, 0)
    compute(1, 0)
    pass_on(2, 1)
    compute(1, 1)
    pass_on(3, 1)
    compute(2, 0)
    compute(3, 0)
    compute(2, 1)
    compute(3, 1)

    for bits in range(1, 16):
        to_wide(bits).wait_send()
    for source in range(16):
        across(source).wait_send()
    switch_copy.wait_send()


def paired_body(*operands):
    charges, leaf_angle, lagrange = operands[:3]
    points, columns = charges.shape
    rank = lagrange.shape[0]
    per_box = columns // leaf_angle.shape[1]
    operands = operands[:-1] + (operands[-1].T,)
    return pl.pallas_call(
        functools.partial(kernel, per_box),
        out_shape=pltpu.VMEM((points, columns), BF16),
        in_specs=[pl.BlockSpec(memory_space=pltpu.HBM)] * len(operands),
        out_specs=pl.BlockSpec(memory_space=pltpu.VMEM),
        scratch_shapes=[pltpu.VMEM(operand.shape, F32) for operand in operands]
        + [
            pltpu.VMEM((16, points + 16, 128), BF16),
            pltpu.VMEM((16, points + 16, 128), BF16),
            pltpu.VMEM((16, points + 16, 128), BF16),
            pltpu.VMEM((rank, 128), F32),
            pltpu.VMEM((2 * rank + points, columns), F32),
            pltpu.VMEM((2 * rank + points, columns), F32),
            pltpu.VMEM((rank, columns), F32),
            pltpu.VMEM((rank, columns), F32),
            pltpu.SemaphoreType.DMA((16,)),
            pltpu.SemaphoreType.DMA((16,)),
            pltpu.SemaphoreType.DMA((16,)),
            pltpu.SemaphoreType.DMA((16,)),
            pltpu.SemaphoreType.DMA((2,)),
            pltpu.SemaphoreType.DMA((len(operands),)),
        ],
        compiler_params=pltpu.CompilerParams(
            collective_id=0, has_side_effects=True, vmem_limit_bytes=58 * 1024 * 1024
        ),
        cost_estimate=pl.CostEstimate(
            flops=2 * 60000 * 2 * columns, bytes_accessed=4 * points * columns, transcendentals=0
        ),
    )(*operands)


def fits_pairs(mesh, charges, leaf_angle, lagrange):
    devices = mesh.shape["wide"] * mesh.shape["narrow"]
    columns = charges.shape[1] // devices
    boxes = leaf_angle.shape[1] // devices
    return (
        mesh.shape["narrow"] == 2
        and mesh.shape["wide"] == 16
        and columns == 2048
        and boxes == 128
        and charges.shape[0] % 16 == 0
        and lagrange.shape[0] % 16 == 0
        and charges.shape[0] + lagrange.shape[0] <= 128
    )


def solution(mesh):
    def program(charges, leaf_angle, lagrange, *rest):
        fits = fits_pairs(mesh, charges, leaf_angle, lagrange)
        return jax.shard_map(
            paired_body if fits else staged_body,
            mesh=mesh,
            in_specs=(
                P(None, ("wide", "narrow")),
                P(None, ("wide", "narrow")),
                P(),
                P(None, None, ("wide", "narrow")),
                P(),
                P(),
                P(None, ("wide", "narrow")),
                P(),
                P(None, ("wide", "narrow")),
                P(),
            ),
            out_specs=P(None, ("wide", "narrow")),
            check_vma=False,
        )(charges, leaf_angle, lagrange, *rest)

    return program
```

```python
import functools

import jax
import jax.numpy as jnp
from jax import lax
from jax.experimental import pallas as pl
from jax.experimental.pallas import tpu as pltpu
from jax.sharding import PartitionSpec as P

MESH = pl.DeviceIdType.MESH
F32 = jnp.float32
BF16 = jnp.bfloat16


def from_partner(value, axis, apart):
    mask = 2**apart
    pairs = [(source, source ^ mask) for source in range(lax.axis_size(axis))]
    return lax.ppermute(value, axis, pairs)


def product(left, right):
    return jnp.dot(left, right, precision=lax.Precision.HIGHEST, preferred_element_type=jnp.float32)


def rotate(boxes_state, phase_angle, per_box):
    rank = phase_angle.shape[0]
    cos_part = jnp.repeat(jnp.cos(phase_angle), per_box, axis=1)
    sin_part = jnp.repeat(jnp.sin(phase_angle), per_box, axis=1)
    real_part = boxes_state[:rank]
    imag_part = boxes_state[rank:]
    return jnp.concatenate(
        [cos_part * real_part - sin_part * imag_part, sin_part * real_part + cos_part * imag_part],
        axis=0,
    )


def butterfly_level(boxes_state, self_matrix, peer_matrix, phase_angle, bit, per_box):
    sent_state = boxes_state.astype(jnp.bfloat16)
    received = from_partner(sent_state, "narrow", bit)
    combined = product(self_matrix, boxes_state) + product(
        peer_matrix, received.astype(jnp.float32)
    )
    return rotate(combined, phase_angle, per_box)


def leaf_weights(lagrange, point_charges, point_angle, per_box):
    cos_leaf = jnp.repeat(jnp.cos(point_angle), per_box, axis=1)
    sin_leaf = jnp.repeat(jnp.sin(point_angle), per_box, axis=1)
    return jnp.concatenate(
        [product(lagrange, cos_leaf * point_charges), product(lagrange, sin_leaf * point_charges)],
        axis=0,
    )


def staged_body(
    charges,
    leaf_angle,
    lagrange,
    level_angle,
    level_self,
    level_peer,
    switch_angle,
    switch_matrix,
    out_angle,
    evaluate,
):
    per_box = charges.shape[1] // leaf_angle.shape[1]
    rank = lagrange.shape[0]
    last_bit = lax.axis_size("narrow").bit_length() - 2
    boxes_state = leaf_weights(lagrange, charges, leaf_angle, per_box)
    boxes_state = butterfly_level(
        boxes_state, level_self[0], level_peer[0], level_angle[0], 0, per_box
    )
    boxes_state = lax.all_to_all(boxes_state, "wide", split_axis=1, concat_axis=1, tiled=True)
    boxes_state = rotate(product(switch_matrix, boxes_state), switch_angle, per_box)
    boxes_state = butterfly_level(
        boxes_state, level_self[1], level_peer[1], level_angle[1], last_bit, per_box
    )
    real_part = product(evaluate, boxes_state[:rank])
    imag_part = product(evaluate, boxes_state[rank:])
    cos_out = jnp.repeat(jnp.cos(out_angle), per_box, axis=1)
    sin_out = jnp.repeat(jnp.sin(out_angle), per_box, axis=1)
    return (cos_out * real_part - sin_out * imag_part).astype(jnp.bfloat16)


def cos_sin(angle):
    half = angle * 0.5
    t = half * half
    s = half * (
        1.0
        + t * (-1 / 6 + t * (1 / 120 + t * (-1 / 5040 + t * (1 / 362880 + t * (-1 / 39916800)))))
    )
    c = 1.0 + t * (
        -1 / 2
        + t * (1 / 24 + t * (-1 / 720 + t * (1 / 40320 + t * (-1 / 3628800 + t / 479001600))))
    )
    return 1.0 - 2.0 * s * s, 2.0 * s * c


def split(value):
    high = value.astype(BF16)
    return high, (value - high.astype(F32)).astype(BF16)


def dot(left, right):
    return jnp.dot(left, right, preferred_element_type=F32)


def spread(boxes, columns, first, per_box):
    box = lax.broadcasted_iota(jnp.int32, (boxes, columns), 0)
    column = lax.broadcasted_iota(jnp.int32, (boxes, columns), 1) + first * per_box
    low = box * per_box
    once = jnp.where((column >= low) & (column < low + per_box), 1.0, 0.0).astype(BF16)
    return jnp.concatenate([once, once], axis=0)


def flip(index, bits):
    if bits == 0:
        return index
    if bits == 1:
        return index + 1 - 2 * lax.rem(index, 2)
    if bits == 2:
        return lax.rem(index + 2, 4)
    return 3 - index


def turn(real, imag, cos_part, sin_part):
    return cos_part * real - sin_part * imag, sin_part * real + cos_part * imag


def kernel(
    per_box,
    *refs,
):
    given, refs = refs[:10], refs[10:]
    field, (held, refs) = refs[0], (refs[1:11], refs[11:])
    (
        charges,
        leaf_angle,
        lagrange,
        level_angle,
        level_self,
        level_peer,
        switch_angle,
        switch_matrix,
        out_angle,
        evaluate,
    ) = held
    (
    outbox,
    own,
    peer,
    peer_switch,
    cos_table,
    sin_table,
    cos_peer,
    sin_peer,
    wide_send,
    wide_recv,
    narrow_send,
    narrow_recv,
    switch_sems,
    load_sems,
    ) = refs
    loads = [pltpu.make_async_copy(g, h, load_sems.at[i]) for i, (g, h) in enumerate(zip(given, held))]
    first_loads = [1, 3, 0, 6]
    later_loads = [i for i in range(10) if i not in first_loads]
    for i in first_loads + later_loads:
        loads[i].start()
    me = lax.axis_index("wide")
    row = lax.axis_index("narrow")
    layer = me // 4
    place = lax.rem(me, 4)
    other = 1 - row
    rank, points = lagrange.shape
    angles = points + rank

    barrier = pltpu.get_barrier_semaphore()
    for bits in range(1, 16):
        to = flip(layer, bits // 4) * 4 + flip(place, bits % 4)
        pl.semaphore_signal(barrier, inc=1, device_id={"wide": to}, device_id_type=MESH)
    pl.semaphore_signal(barrier, inc=1, device_id={"narrow": other}, device_id_type=MESH)

    for i in first_loads:
        loads[i].wait()

    stacked = jnp.concatenate(
        [leaf_angle[...], level_angle[0], jnp.zeros((128 - angles, 128), F32)], axis=0
    )
    by_box = stacked.T
    high = by_box.astype(BF16).astype(F32)
    low = by_box - high
    for to in range(16):
        outbox[to, :points, :] = charges[:, to * 128 : (to + 1) * 128].astype(BF16)
        pair = jnp.concatenate([high[to * 8 : to * 8 + 8], low[to * 8 : to * 8 + 8]], axis=0)
        outbox[to, points : points + 16, :] = pair.astype(BF16)
    own[me] = outbox[me]

    def to_wide(bits):
        to = flip(layer, bits // 4) * 4 + flip(place, bits % 4)
        return pltpu.make_async_remote_copy(
            src_ref=outbox.at[to],
            dst_ref=own.at[me],
            send_sem=wide_send.at[to],
            recv_sem=wide_recv.at[me],
            device_id={"wide": to},
            device_id_type=MESH,
        )

    def from_wide(source):
        return pltpu.make_async_remote_copy(
            src_ref=outbox.at[source],
            dst_ref=own.at[source],
            send_sem=wide_send.at[source],
            recv_sem=wide_recv.at[source],
            device_id={"wide": source},
            device_id_type=MESH,
        )

    def across(source):
        return pltpu.make_async_remote_copy(
            src_ref=own.at[source],
            dst_ref=peer.at[source],
            send_sem=narrow_send.at[source],
            recv_sem=narrow_recv.at[source],
            device_id={"narrow": other},
            device_id_type=MESH,
        )

    switch_copy = pltpu.make_async_remote_copy(
        src_ref=switch_angle,
        dst_ref=peer_switch,
        send_sem=switch_sems.at[0],
        recv_sem=switch_sems.at[1],
        device_id={"narrow": other},
        device_id_type=MESH,
    )

    pl.semaphore_wait(barrier, 16)
    across(me).start()
    order = [1, 8, 2, 9, 4, 10, 3, 11, 5, 12, 6, 13, 7, 14, 15]
    for bits in order:
        to_wide(bits).start()
    switch_copy.start()

    def pass_on(group):
        for bits in range(4):
            if group or bits:
                source = flip(layer, group) * 4 + flip(place, bits)
                from_wide(source).wait_recv()
                across(source).start()

    for i in later_loads:
        loads[i].wait()

    fill_columns = 4 * 128
    group_columns = 8 * 128

    def fill(angle, first_row, cos_to, sin_to):
        rows = angle.shape[0]
        both = jnp.concatenate(cos_sin(angle), axis=0)
        halves = jnp.concatenate(split(both), axis=1)
        for group in range(4):
            columns = pl.ds(group * fill_columns, fill_columns)
            wide = dot(halves, spread(128, fill_columns, group * fill_columns // per_box, per_box))
            cos_to[pl.ds(first_row, rows), columns] = wide[:rows]
            sin_to[pl.ds(first_row, rows), columns] = wide[rows:]

    local = jnp.concatenate([switch_angle[...], level_angle[1], out_angle[...]], axis=0)
    fill(local, 0, cos_table, sin_table)

    lag_high, lag_low = split(lagrange[...])
    leaf_matrix = jnp.concatenate([lag_high, lag_low], axis=1)
    eva_high, eva_low = split(evaluate[...].T)
    out_matrix = jnp.concatenate([eva_high, eva_low, eva_high], axis=1)
    both_matrix = split(
        jnp.concatenate(
            [
                jnp.concatenate([level_self[0], level_peer[0]], axis=1),
                jnp.concatenate([level_peer[0], level_self[0]], axis=1),
            ],
            axis=0,
        )
    )
    both_matrix = jnp.concatenate(both_matrix, axis=0)
    swi_high, swi_low = split(switch_matrix[...])
    swi_matrix = jnp.concatenate([swi_high, swi_low], axis=1)
    last_matrix = split(jnp.concatenate([level_self[1], level_peer[1]], axis=1))
    last_matrix = jnp.concatenate(last_matrix, axis=0)
    repeat = spread(64, group_columns, 0, per_box)

    def leaf(box, sources):
        charge = jnp.concatenate([box[source, :points, :] for source in sources], axis=1).astype(F32)
        parts = [box[source, points : points + 16, :].astype(F32) for source in sources]
        angle = jnp.concatenate([part[:8] + part[8:] for part in parts], axis=0)
        both = jnp.concatenate(cos_sin(angle), axis=1)
        halves = jnp.concatenate(split(both), axis=0)
        wide = lax.dot_general(
            halves, repeat, (((0,), (0,)), ((), ())), preferred_element_type=F32
        )
        cos_part, sin_part = wide[:128], wide[128:]
        weighted = jnp.concatenate([cos_part[:points] * charge, sin_part[:points] * charge], axis=1)
        weighted = weighted.astype(BF16)
        state = dot(leaf_matrix, jnp.concatenate([weighted, weighted], axis=0))
        turned = cos_part[points:angles], sin_part[points:angles]
        return [state[:, :group_columns], state[:, group_columns:]], turned

    def compute(groups):
        wheres = [flip(layer, group) for group in groups]
        sources = [where * 4 + i for where in wheres for i in range(4)]
        blocks = [pl.ds(pl.multiple_of(where * 512, 512), 512) for where in wheres]

        def table(values, start, rows):
            return jnp.concatenate(
                [values[start : start + rows, block] for block in blocks], axis=1
            )

        state_own, turn_own = leaf(own, sources)
        for source in sources:
            across(source).wait_recv()
        state_peer, turn_peer = leaf(peer, sources)
        state = jnp.concatenate(state_own + state_peer, axis=0).astype(BF16)
        first = dot(both_matrix, state)
        first = first[: 4 * rank] + first[4 * rank :]
        own_real, own_imag = turn(first[:rank], first[rank : 2 * rank], *turn_own)
        peer_real, peer_imag = turn(first[2 * rank : 3 * rank], first[3 * rank :], *turn_peer)
        moved = jnp.concatenate(
            [
                jnp.concatenate([own_real, peer_real], axis=1),
                jnp.concatenate([own_imag, peer_imag], axis=1),
            ],
            axis=0,
        ).astype(BF16)
        middle = dot(swi_matrix, jnp.concatenate([moved, moved], axis=0))
        own_real, own_imag = turn(
            middle[:rank, :group_columns],
            middle[rank:, :group_columns],
            table(cos_table, 0, rank),
            table(sin_table, 0, rank),
        )
        peer_real, peer_imag = turn(
            middle[:rank, group_columns:],
            middle[rank:, group_columns:],
            table(cos_peer, 0, rank),
            table(sin_peer, 0, rank),
        )
        state = jnp.concatenate([own_real, own_imag, peer_real, peer_imag], axis=0).astype(BF16)
        last = dot(last_matrix, state)
        last = last[: 2 * rank] + last[2 * rank :]
        real, imag = turn(
            last[:rank],
            last[rank:],
            table(cos_table, rank, rank),
            table(sin_table, rank, rank),
        )
        high, low = split(jnp.concatenate([real, imag], axis=1))
        value = dot(out_matrix, jnp.concatenate([high, high, low], axis=0))
        result = (
            table(cos_table, 2 * rank, points) * value[:, :group_columns]
            - table(sin_table, 2 * rank, points) * value[:, group_columns:]
        ).astype(BF16)
        for i, block in enumerate(blocks):
            field[:, block] = result[:, i * 512 : (i + 1) * 512]

    pass_on(0)
    pass_on(1)
    switch_copy.wait_recv()
    fill(peer_switch[...], 0, cos_peer, sin_peer)
    pass_on(2)
    compute((0, 1))
    pass_on(3)
    compute((2, 3))

    for bits in range(1, 16):
        to_wide(bits).wait_send()
    for source in range(16):
        across(source).wait_send()
    switch_copy.wait_send()


def paired_body(*operands):
    charges, leaf_angle, lagrange = operands[:3]
    points, columns = charges.shape
    rank = lagrange.shape[0]
    per_box = columns // leaf_angle.shape[1]
    operands = operands[:-1] + (operands[-1].T,)
    return pl.pallas_call(
        functools.partial(kernel, per_box),
        out_shape=pltpu.VMEM((points, columns), BF16),
        in_specs=[pl.BlockSpec(memory_space=pltpu.HBM)] * len(operands),
        out_specs=pl.BlockSpec(memory_space=pltpu.VMEM),
        scratch_shapes=[pltpu.VMEM(operand.shape, F32) for operand in operands]
        + [
            pltpu.VMEM((16, points + 16, 128), BF16),
            pltpu.VMEM((16, points + 16, 128), BF16),
            pltpu.VMEM((16, points + 16, 128), BF16),
            pltpu.VMEM((rank, 128), F32),
            pltpu.VMEM((2 * rank + points, columns), F32),
            pltpu.VMEM((2 * rank + points, columns), F32),
            pltpu.VMEM((rank, columns), F32),
            pltpu.VMEM((rank, columns), F32),
            pltpu.SemaphoreType.DMA((16,)),
            pltpu.SemaphoreType.DMA((16,)),
            pltpu.SemaphoreType.DMA((16,)),
            pltpu.SemaphoreType.DMA((16,)),
            pltpu.SemaphoreType.DMA((2,)),
            pltpu.SemaphoreType.DMA((len(operands),)),
        ],
        compiler_params=pltpu.CompilerParams(
            collective_id=0, has_side_effects=True, vmem_limit_bytes=58 * 1024 * 1024
        ),
        cost_estimate=pl.CostEstimate(
            flops=2 * 60000 * 2 * columns, bytes_accessed=4 * points * columns, transcendentals=0
        ),
    )(*operands)


def fits_pairs(mesh, charges, leaf_angle, lagrange):
    devices = mesh.shape["wide"] * mesh.shape["narrow"]
    columns = charges.shape[1] // devices
    boxes = leaf_angle.shape[1] // devices
    return (
        mesh.shape["narrow"] == 2
        and mesh.shape["wide"] == 16
        and columns == 2048
        and boxes == 128
        and charges.shape[0] % 16 == 0
        and lagrange.shape[0] % 16 == 0
        and charges.shape[0] + lagrange.shape[0] <= 128
    )


def solution(mesh):
    def program(charges, leaf_angle, lagrange, *rest):
        fits = fits_pairs(mesh, charges, leaf_angle, lagrange)
        return jax.shard_map(
            paired_body if fits else staged_body,
            mesh=mesh,
            in_specs=(
                P(None, ("wide", "narrow")),
                P(None, ("wide", "narrow")),
                P(),
                P(None, None, ("wide", "narrow")),
                P(),
                P(),
                P(None, ("wide", "narrow")),
                P(),
                P(None, ("wide", "narrow")),
                P(),
            ),
            out_specs=P(None, ("wide", "narrow")),
            check_vma=False,
        )(charges, leaf_angle, lagrange, *rest)

    return program
```

```python
import functools

import jax
import jax.numpy as jnp
from jax import lax
from jax.experimental import pallas as pl
from jax.experimental.pallas import tpu as pltpu
from jax.sharding import PartitionSpec as P

MESH = pl.DeviceIdType.MESH
F32 = jnp.float32
BF16 = jnp.bfloat16


def from_partner(value, axis, apart):
    mask = 2**apart
    pairs = [(source, source ^ mask) for source in range(lax.axis_size(axis))]
    return lax.ppermute(value, axis, pairs)


def product(left, right):
    return jnp.dot(left, right, precision=lax.Precision.HIGHEST, preferred_element_type=jnp.float32)


def rotate(boxes_state, phase_angle, per_box):
    rank = phase_angle.shape[0]
    cos_part = jnp.repeat(jnp.cos(phase_angle), per_box, axis=1)
    sin_part = jnp.repeat(jnp.sin(phase_angle), per_box, axis=1)
    real_part = boxes_state[:rank]
    imag_part = boxes_state[rank:]
    return jnp.concatenate(
        [cos_part * real_part - sin_part * imag_part, sin_part * real_part + cos_part * imag_part],
        axis=0,
    )


def butterfly_level(boxes_state, self_matrix, peer_matrix, phase_angle, bit, per_box):
    sent_state = boxes_state.astype(jnp.bfloat16)
    received = from_partner(sent_state, "narrow", bit)
    combined = product(self_matrix, boxes_state) + product(
        peer_matrix, received.astype(jnp.float32)
    )
    return rotate(combined, phase_angle, per_box)


def leaf_weights(lagrange, point_charges, point_angle, per_box):
    cos_leaf = jnp.repeat(jnp.cos(point_angle), per_box, axis=1)
    sin_leaf = jnp.repeat(jnp.sin(point_angle), per_box, axis=1)
    return jnp.concatenate(
        [product(lagrange, cos_leaf * point_charges), product(lagrange, sin_leaf * point_charges)],
        axis=0,
    )


def staged_body(
    charges,
    leaf_angle,
    lagrange,
    level_angle,
    level_self,
    level_peer,
    switch_angle,
    switch_matrix,
    out_angle,
    evaluate,
):
    per_box = charges.shape[1] // leaf_angle.shape[1]
    rank = lagrange.shape[0]
    last_bit = lax.axis_size("narrow").bit_length() - 2
    boxes_state = leaf_weights(lagrange, charges, leaf_angle, per_box)
    boxes_state = butterfly_level(
        boxes_state, level_self[0], level_peer[0], level_angle[0], 0, per_box
    )
    boxes_state = lax.all_to_all(boxes_state, "wide", split_axis=1, concat_axis=1, tiled=True)
    boxes_state = rotate(product(switch_matrix, boxes_state), switch_angle, per_box)
    boxes_state = butterfly_level(
        boxes_state, level_self[1], level_peer[1], level_angle[1], last_bit, per_box
    )
    real_part = product(evaluate, boxes_state[:rank])
    imag_part = product(evaluate, boxes_state[rank:])
    cos_out = jnp.repeat(jnp.cos(out_angle), per_box, axis=1)
    sin_out = jnp.repeat(jnp.sin(out_angle), per_box, axis=1)
    return (cos_out * real_part - sin_out * imag_part).astype(jnp.bfloat16)


def cos_sin(angle):
    half = angle * 0.5
    t = half * half
    s = half * (
        1.0
        + t * (-1 / 6 + t * (1 / 120 + t * (-1 / 5040 + t * (1 / 362880 + t * (-1 / 39916800)))))
    )
    c = 1.0 + t * (
        -1 / 2
        + t * (1 / 24 + t * (-1 / 720 + t * (1 / 40320 + t * (-1 / 3628800 + t / 479001600))))
    )
    return 1.0 - 2.0 * s * s, 2.0 * s * c


def split(value):
    high = value.astype(BF16)
    return high, (value - high.astype(F32)).astype(BF16)


def dot(left, right):
    return jnp.dot(left, right, preferred_element_type=F32)


def spread(boxes, columns, first, per_box):
    box = lax.broadcasted_iota(jnp.int32, (boxes, columns), 0)
    column = lax.broadcasted_iota(jnp.int32, (boxes, columns), 1) + first * per_box
    low = box * per_box
    once = jnp.where((column >= low) & (column < low + per_box), 1.0, 0.0).astype(BF16)
    return jnp.concatenate([once, once], axis=0)


def flip(index, bits):
    if bits == 0:
        return index
    if bits == 1:
        return index + 1 - 2 * lax.rem(index, 2)
    if bits == 2:
        return lax.rem(index + 2, 4)
    return 3 - index


def turn(real, imag, cos_part, sin_part):
    return cos_part * real - sin_part * imag, sin_part * real + cos_part * imag


def kernel(
    per_box,
    *refs,
):
    given, refs = refs[:10], refs[10:]
    field, (held, refs) = refs[0], (refs[1:11], refs[11:])
    (
        charges,
        leaf_angle,
        lagrange,
        level_angle,
        level_self,
        level_peer,
        switch_angle,
        switch_matrix,
        out_angle,
        evaluate,
    ) = held
    (
    outbox,
    own,
    peer,
    peer_switch,
    cos_table,
    sin_table,
    cos_peer,
    sin_peer,
    wide_send,
    wide_recv,
    narrow_send,
    narrow_recv,
    switch_sems,
    load_sems,
    ) = refs
    loads = [pltpu.make_async_copy(g, h, load_sems.at[i]) for i, (g, h) in enumerate(zip(given, held))]
    first_loads = [1, 3, 0, 6]
    later_loads = [i for i in range(10) if i not in first_loads]
    for i in first_loads + later_loads:
        loads[i].start()
    me = lax.axis_index("wide")
    row = lax.axis_index("narrow")
    layer = me // 4
    place = lax.rem(me, 4)
    other = 1 - row
    rank, points = lagrange.shape
    angles = points + rank

    barrier = pltpu.get_barrier_semaphore()
    for bits in range(1, 16):
        to = flip(layer, bits // 4) * 4 + flip(place, bits % 4)
        pl.semaphore_signal(barrier, inc=1, device_id={"wide": to}, device_id_type=MESH)
    pl.semaphore_signal(barrier, inc=1, device_id={"narrow": other}, device_id_type=MESH)

    for i in first_loads:
        loads[i].wait()

    stacked = jnp.concatenate(
        [leaf_angle[...], level_angle[0], jnp.zeros((128 - angles, 128), F32)], axis=0
    )
    by_box = stacked.T
    high = by_box.astype(BF16).astype(F32)
    low = by_box - high
    for to in range(16):
        outbox[to, :points, :] = charges[:, to * 128 : (to + 1) * 128].astype(BF16)
        pair = jnp.concatenate([high[to * 8 : to * 8 + 8], low[to * 8 : to * 8 + 8]], axis=0)
        outbox[to, points : points + 16, :] = pair.astype(BF16)
    own[me] = outbox[me]

    def to_wide(bits):
        to = flip(layer, bits // 4) * 4 + flip(place, bits % 4)
        return pltpu.make_async_remote_copy(
            src_ref=outbox.at[to],
            dst_ref=own.at[me],
            send_sem=wide_send.at[to],
            recv_sem=wide_recv.at[me],
            device_id={"wide": to},
            device_id_type=MESH,
        )

    def from_wide(source):
        return pltpu.make_async_remote_copy(
            src_ref=outbox.at[source],
            dst_ref=own.at[source],
            send_sem=wide_send.at[source],
            recv_sem=wide_recv.at[source],
            device_id={"wide": source},
            device_id_type=MESH,
        )

    def across(source):
        return pltpu.make_async_remote_copy(
            src_ref=own.at[source],
            dst_ref=peer.at[source],
            send_sem=narrow_send.at[source],
            recv_sem=narrow_recv.at[source],
            device_id={"narrow": other},
            device_id_type=MESH,
        )

    switch_copy = pltpu.make_async_remote_copy(
        src_ref=switch_angle,
        dst_ref=peer_switch,
        send_sem=switch_sems.at[0],
        recv_sem=switch_sems.at[1],
        device_id={"narrow": other},
        device_id_type=MESH,
    )

    pl.semaphore_wait(barrier, 16)
    across(me).start()
    order = [1, 8, 2, 9, 4, 10, 3, 11, 5, 12, 6, 13, 7, 14, 15]
    for bits in order:
        to_wide(bits).start()
    switch_copy.start()

    def pass_on(group):
        for bits in range(4):
            if group or bits:
                source = flip(layer, group) * 4 + flip(place, bits)
                from_wide(source).wait_recv()
                across(source).start()

    for i in later_loads:
        loads[i].wait()

    fill_columns = 4 * 128

    def fill(angle, first_row, cos_to, sin_to):
        rows = angle.shape[0]
        both = jnp.concatenate(cos_sin(angle), axis=0)
        halves = jnp.concatenate(split(both), axis=1)
        for group in range(4):
            columns = pl.ds(group * fill_columns, fill_columns)
            wide = dot(halves, spread(128, fill_columns, group * fill_columns // per_box, per_box))
            cos_to[pl.ds(first_row, rows), columns] = wide[:rows]
            sin_to[pl.ds(first_row, rows), columns] = wide[rows:]


    lag_high, lag_low = split(lagrange[...])
    leaf_matrix = jnp.concatenate([lag_high, lag_low], axis=1)
    eva_high, eva_low = split(evaluate[...].T)
    out_matrix = jnp.concatenate([eva_high, eva_low, eva_high], axis=1)
    both_matrix = split(
        jnp.concatenate(
            [
                jnp.concatenate([level_self[0], level_peer[0]], axis=1),
                jnp.concatenate([level_peer[0], level_self[0]], axis=1),
            ],
            axis=0,
        )
    )
    both_matrix = jnp.concatenate(both_matrix, axis=0)
    swi_high, swi_low = split(switch_matrix[...])
    swi_matrix = jnp.concatenate([swi_high, swi_low], axis=1)
    last_matrix = split(jnp.concatenate([level_self[1], level_peer[1]], axis=1))
    last_matrix = jnp.concatenate(last_matrix, axis=0)

    def leaf(box, sources):
        group_columns = 128 * len(sources)
        repeat = spread(8 * len(sources), group_columns, 0, per_box)
        charge = jnp.concatenate([box[source, :points, :] for source in sources], axis=1).astype(F32)
        parts = [box[source, points : points + 16, :].astype(F32) for source in sources]
        angle = jnp.concatenate([part[:8] + part[8:] for part in parts], axis=0)
        both = jnp.concatenate(cos_sin(angle), axis=1)
        halves = jnp.concatenate(split(both), axis=0)
        wide = lax.dot_general(
            halves, repeat, (((0,), (0,)), ((), ())), preferred_element_type=F32
        )
        cos_part, sin_part = wide[:128], wide[128:]
        weighted = jnp.concatenate([cos_part[:points] * charge, sin_part[:points] * charge], axis=1)
        weighted = weighted.astype(BF16)
        state = dot(leaf_matrix, jnp.concatenate([weighted, weighted], axis=0))
        turned = cos_part[points:angles], sin_part[points:angles]
        return [state[:, :group_columns], state[:, group_columns:]], turned

    def compute(groups, meanwhile=None):
        group_columns = 512 * len(groups)
        wheres = [flip(layer, group) for group in groups]
        sources = [where * 4 + i for where in wheres for i in range(4)]
        blocks = [pl.ds(pl.multiple_of(where * 512, 512), 512) for where in wheres]

        def table(values, start, rows):
            return jnp.concatenate(
                [values[start : start + rows, block] for block in blocks], axis=1
            )

        state_own, turn_own = leaf(own, sources)
        if meanwhile is not None:
            pass_on(meanwhile)
        for source in sources:
            across(source).wait_recv()
        state_peer, turn_peer = leaf(peer, sources)
        state = jnp.concatenate(state_own + state_peer, axis=0).astype(BF16)
        first = dot(both_matrix, state)
        first = first[: 4 * rank] + first[4 * rank :]
        own_real, own_imag = turn(first[:rank], first[rank : 2 * rank], *turn_own)
        peer_real, peer_imag = turn(first[2 * rank : 3 * rank], first[3 * rank :], *turn_peer)
        moved = jnp.concatenate(
            [
                jnp.concatenate([own_real, peer_real], axis=1),
                jnp.concatenate([own_imag, peer_imag], axis=1),
            ],
            axis=0,
        ).astype(BF16)
        middle = dot(swi_matrix, jnp.concatenate([moved, moved], axis=0))
        own_real, own_imag = turn(
            middle[:rank, :group_columns],
            middle[rank:, :group_columns],
            table(cos_table, 0, rank),
            table(sin_table, 0, rank),
        )
        peer_real, peer_imag = turn(
            middle[:rank, group_columns:],
            middle[rank:, group_columns:],
            table(cos_peer, 0, rank),
            table(sin_peer, 0, rank),
        )
        state = jnp.concatenate([own_real, own_imag, peer_real, peer_imag], axis=0).astype(BF16)
        last = dot(last_matrix, state)
        last = last[: 2 * rank] + last[2 * rank :]
        real, imag = turn(
            last[:rank],
            last[rank:],
            table(cos_table, rank, rank),
            table(sin_table, rank, rank),
        )
        high, low = split(jnp.concatenate([real, imag], axis=1))
        value = dot(out_matrix, jnp.concatenate([high, high, low], axis=0))
        result = (
            table(cos_table, 2 * rank, points) * value[:, :group_columns]
            - table(sin_table, 2 * rank, points) * value[:, group_columns:]
        ).astype(BF16)
        for i, block in enumerate(blocks):
            field[:, block] = result[:, i * 512 : (i + 1) * 512]

    pass_on(0)
    local = jnp.concatenate([switch_angle[...], level_angle[1], out_angle[...]], axis=0)
    fill(local, 0, cos_table, sin_table)
    pass_on(1)
    switch_copy.wait_recv()
    fill(peer_switch[...], 0, cos_peer, sin_peer)
    compute((0, 1), 2)
    compute((2,), 3)
    compute((3,))

    for bits in range(1, 16):
        to_wide(bits).wait_send()
    for source in range(16):
        across(source).wait_send()
    switch_copy.wait_send()


def paired_body(*operands):
    charges, leaf_angle, lagrange = operands[:3]
    points, columns = charges.shape
    rank = lagrange.shape[0]
    per_box = columns // leaf_angle.shape[1]
    operands = operands[:-1] + (operands[-1].T,)
    return pl.pallas_call(
        functools.partial(kernel, per_box),
        out_shape=pltpu.VMEM((points, columns), BF16),
        in_specs=[pl.BlockSpec(memory_space=pltpu.HBM)] * len(operands),
        out_specs=pl.BlockSpec(memory_space=pltpu.VMEM),
        scratch_shapes=[pltpu.VMEM(operand.shape, F32) for operand in operands]
        + [
            pltpu.VMEM((16, points + 16, 128), BF16),
            pltpu.VMEM((16, points + 16, 128), BF16),
            pltpu.VMEM((16, points + 16, 128), BF16),
            pltpu.VMEM((rank, 128), F32),
            pltpu.VMEM((2 * rank + points, columns), F32),
            pltpu.VMEM((2 * rank + points, columns), F32),
            pltpu.VMEM((rank, columns), F32),
            pltpu.VMEM((rank, columns), F32),
            pltpu.SemaphoreType.DMA((16,)),
            pltpu.SemaphoreType.DMA((16,)),
            pltpu.SemaphoreType.DMA((16,)),
            pltpu.SemaphoreType.DMA((16,)),
            pltpu.SemaphoreType.DMA((2,)),
            pltpu.SemaphoreType.DMA((len(operands),)),
        ],
        compiler_params=pltpu.CompilerParams(
            collective_id=0, has_side_effects=True, vmem_limit_bytes=58 * 1024 * 1024
        ),
        cost_estimate=pl.CostEstimate(
            flops=2 * 60000 * 2 * columns, bytes_accessed=4 * points * columns, transcendentals=0
        ),
    )(*operands)


def fits_pairs(mesh, charges, leaf_angle, lagrange):
    devices = mesh.shape["wide"] * mesh.shape["narrow"]
    columns = charges.shape[1] // devices
    boxes = leaf_angle.shape[1] // devices
    return (
        mesh.shape["narrow"] == 2
        and mesh.shape["wide"] == 16
        and columns == 2048
        and boxes == 128
        and charges.shape[0] % 16 == 0
        and lagrange.shape[0] % 16 == 0
        and charges.shape[0] + lagrange.shape[0] <= 128
    )


def solution(mesh):
    def program(charges, leaf_angle, lagrange, *rest):
        fits = fits_pairs(mesh, charges, leaf_angle, lagrange)
        return jax.shard_map(
            paired_body if fits else staged_body,
            mesh=mesh,
            in_specs=(
                P(None, ("wide", "narrow")),
                P(None, ("wide", "narrow")),
                P(),
                P(None, None, ("wide", "narrow")),
                P(),
                P(),
                P(None, ("wide", "narrow")),
                P(),
                P(None, ("wide", "narrow")),
                P(),
            ),
            out_specs=P(None, ("wide", "narrow")),
            check_vma=False,
        )(charges, leaf_angle, lagrange, *rest)

    return program
```

```python
import functools

import jax
import jax.numpy as jnp
from jax import lax
from jax.experimental import pallas as pl
from jax.experimental.pallas import tpu as pltpu
from jax.sharding import PartitionSpec as P

MESH = pl.DeviceIdType.MESH
F32 = jnp.float32
BF16 = jnp.bfloat16


def from_partner(value, axis, apart):
    mask = 2**apart
    pairs = [(source, source ^ mask) for source in range(lax.axis_size(axis))]
    return lax.ppermute(value, axis, pairs)


def product(left, right):
    return jnp.dot(left, right, precision=lax.Precision.HIGHEST, preferred_element_type=jnp.float32)


def rotate(boxes_state, phase_angle, per_box):
    rank = phase_angle.shape[0]
    cos_part = jnp.repeat(jnp.cos(phase_angle), per_box, axis=1)
    sin_part = jnp.repeat(jnp.sin(phase_angle), per_box, axis=1)
    real_part = boxes_state[:rank]
    imag_part = boxes_state[rank:]
    return jnp.concatenate(
        [cos_part * real_part - sin_part * imag_part, sin_part * real_part + cos_part * imag_part],
        axis=0,
    )


def butterfly_level(boxes_state, self_matrix, peer_matrix, phase_angle, bit, per_box):
    sent_state = boxes_state.astype(jnp.bfloat16)
    received = from_partner(sent_state, "narrow", bit)
    combined = product(self_matrix, boxes_state) + product(
        peer_matrix, received.astype(jnp.float32)
    )
    return rotate(combined, phase_angle, per_box)


def leaf_weights(lagrange, point_charges, point_angle, per_box):
    cos_leaf = jnp.repeat(jnp.cos(point_angle), per_box, axis=1)
    sin_leaf = jnp.repeat(jnp.sin(point_angle), per_box, axis=1)
    return jnp.concatenate(
        [product(lagrange, cos_leaf * point_charges), product(lagrange, sin_leaf * point_charges)],
        axis=0,
    )


def staged_body(
    charges,
    leaf_angle,
    lagrange,
    level_angle,
    level_self,
    level_peer,
    switch_angle,
    switch_matrix,
    out_angle,
    evaluate,
):
    per_box = charges.shape[1] // leaf_angle.shape[1]
    rank = lagrange.shape[0]
    last_bit = lax.axis_size("narrow").bit_length() - 2
    boxes_state = leaf_weights(lagrange, charges, leaf_angle, per_box)
    boxes_state = butterfly_level(
        boxes_state, level_self[0], level_peer[0], level_angle[0], 0, per_box
    )
    boxes_state = lax.all_to_all(boxes_state, "wide", split_axis=1, concat_axis=1, tiled=True)
    boxes_state = rotate(product(switch_matrix, boxes_state), switch_angle, per_box)
    boxes_state = butterfly_level(
        boxes_state, level_self[1], level_peer[1], level_angle[1], last_bit, per_box
    )
    real_part = product(evaluate, boxes_state[:rank])
    imag_part = product(evaluate, boxes_state[rank:])
    cos_out = jnp.repeat(jnp.cos(out_angle), per_box, axis=1)
    sin_out = jnp.repeat(jnp.sin(out_angle), per_box, axis=1)
    return (cos_out * real_part - sin_out * imag_part).astype(jnp.bfloat16)


def cos_sin(angle):
    half = angle * 0.5
    t = half * half
    s = half * (
        1.0
        + t * (-1 / 6 + t * (1 / 120 + t * (-1 / 5040 + t * (1 / 362880 + t * (-1 / 39916800)))))
    )
    c = 1.0 + t * (
        -1 / 2
        + t * (1 / 24 + t * (-1 / 720 + t * (1 / 40320 + t * (-1 / 3628800 + t / 479001600))))
    )
    return 1.0 - 2.0 * s * s, 2.0 * s * c


def split(value):
    high = value.astype(BF16)
    return high, (value - high.astype(F32)).astype(BF16)


def dot(left, right):
    return jnp.dot(left, right, preferred_element_type=F32)


def spread(boxes, columns, first, per_box):
    box = lax.broadcasted_iota(jnp.int32, (boxes, columns), 0)
    column = lax.broadcasted_iota(jnp.int32, (boxes, columns), 1) + first * per_box
    low = box * per_box
    once = jnp.where((column >= low) & (column < low + per_box), 1.0, 0.0).astype(BF16)
    return jnp.concatenate([once, once], axis=0)


def flip(index, bits):
    if bits == 0:
        return index
    if bits == 1:
        return index + 1 - 2 * lax.rem(index, 2)
    if bits == 2:
        return lax.rem(index + 2, 4)
    return 3 - index


def turn(real, imag, cos_part, sin_part):
    return cos_part * real - sin_part * imag, sin_part * real + cos_part * imag


def kernel(
    per_box,
    *refs,
):
    given, refs = refs[:10], refs[10:]
    field, (held, refs) = refs[0], (refs[1:11], refs[11:])
    (
        charges,
        leaf_angle,
        lagrange,
        level_angle,
        level_self,
        level_peer,
        switch_angle,
        switch_matrix,
        out_angle,
        evaluate,
    ) = held
    (
    outbox,
    own,
    peer,
    peer_switch,
    cos_table,
    sin_table,
    cos_peer,
    sin_peer,
    wide_send,
    wide_recv,
    narrow_send,
    narrow_recv,
    switch_sems,
    load_sems,
    ) = refs
    loads = [pltpu.make_async_copy(g, h, load_sems.at[i]) for i, (g, h) in enumerate(zip(given, held))]
    first_loads = [1, 3, 0, 6]
    later_loads = [i for i in range(10) if i not in first_loads]
    for i in first_loads + later_loads:
        loads[i].start()
    me = lax.axis_index("wide")
    row = lax.axis_index("narrow")
    layer = me // 4
    place = lax.rem(me, 4)
    other = 1 - row
    rank, points = lagrange.shape
    angles = points + rank

    barrier = pltpu.get_barrier_semaphore()
    for bits in range(1, 16):
        to = flip(layer, bits // 4) * 4 + flip(place, bits % 4)
        pl.semaphore_signal(barrier, inc=1, device_id={"wide": to}, device_id_type=MESH)
    pl.semaphore_signal(barrier, inc=1, device_id={"narrow": other}, device_id_type=MESH)

    for i in first_loads:
        loads[i].wait()

    stacked = jnp.concatenate(
        [leaf_angle[...], level_angle[0], jnp.zeros((128 - angles, 128), F32)], axis=0
    )
    by_box = stacked.T
    high = by_box.astype(BF16).astype(F32)
    low = by_box - high
    for to in range(16):
        outbox[to, :points, :] = charges[:, to * 128 : (to + 1) * 128].astype(BF16)
        pair = jnp.concatenate([high[to * 8 : to * 8 + 8], low[to * 8 : to * 8 + 8]], axis=0)
        outbox[to, points : points + 16, :] = pair.astype(BF16)
    own[me] = outbox[me]

    def to_wide(bits):
        to = flip(layer, bits // 4) * 4 + flip(place, bits % 4)
        return pltpu.make_async_remote_copy(
            src_ref=outbox.at[to],
            dst_ref=own.at[me],
            send_sem=wide_send.at[to],
            recv_sem=wide_recv.at[me],
            device_id={"wide": to},
            device_id_type=MESH,
        )

    def from_wide(source):
        return pltpu.make_async_remote_copy(
            src_ref=outbox.at[source],
            dst_ref=own.at[source],
            send_sem=wide_send.at[source],
            recv_sem=wide_recv.at[source],
            device_id={"wide": source},
            device_id_type=MESH,
        )

    def across(source):
        return pltpu.make_async_remote_copy(
            src_ref=own.at[source],
            dst_ref=peer.at[source],
            send_sem=narrow_send.at[source],
            recv_sem=narrow_recv.at[source],
            device_id={"narrow": other},
            device_id_type=MESH,
        )

    switch_copy = pltpu.make_async_remote_copy(
        src_ref=switch_angle,
        dst_ref=peer_switch,
        send_sem=switch_sems.at[0],
        recv_sem=switch_sems.at[1],
        device_id={"narrow": other},
        device_id_type=MESH,
    )

    pl.semaphore_wait(barrier, 16)
    across(me).start()
    def send(order):
        for bits in order:
            to_wide(bits).start()

    send([1, 8, 2, 9, 3, 10, 4, 11, 5])
    switch_copy.start()

    def pass_on(group):
        for bits in range(4):
            if group or bits:
                source = flip(layer, group) * 4 + flip(place, bits)
                from_wide(source).wait_recv()
                across(source).start()

    for i in later_loads:
        loads[i].wait()

    fill_columns = 4 * 128

    def fill(angle, first_row, cos_to, sin_to):
        rows = angle.shape[0]
        both = jnp.concatenate(cos_sin(angle), axis=0)
        halves = jnp.concatenate(split(both), axis=1)
        for group in range(4):
            columns = pl.ds(group * fill_columns, fill_columns)
            wide = dot(halves, spread(128, fill_columns, group * fill_columns // per_box, per_box))
            cos_to[pl.ds(first_row, rows), columns] = wide[:rows]
            sin_to[pl.ds(first_row, rows), columns] = wide[rows:]


    lag_high, lag_low = split(lagrange[...])
    leaf_matrix = jnp.concatenate([lag_high, lag_low], axis=1)
    eva_high, eva_low = split(evaluate[...].T)
    out_matrix = jnp.concatenate([eva_high, eva_low, eva_high], axis=1)
    both_matrix = split(
        jnp.concatenate(
            [
                jnp.concatenate([level_self[0], level_peer[0]], axis=1),
                jnp.concatenate([level_peer[0], level_self[0]], axis=1),
            ],
            axis=0,
        )
    )
    both_matrix = jnp.concatenate(both_matrix, axis=0)
    swi_high, swi_low = split(switch_matrix[...])
    swi_matrix = jnp.concatenate([swi_high, swi_low], axis=1)
    last_matrix = split(jnp.concatenate([level_self[1], level_peer[1]], axis=1))
    last_matrix = jnp.concatenate(last_matrix, axis=0)

    def leaf(box, sources):
        group_columns = 128 * len(sources)
        repeat = spread(8 * len(sources), group_columns, 0, per_box)
        charge = jnp.concatenate([box[source, :points, :] for source in sources], axis=1).astype(F32)
        parts = [box[source, points : points + 16, :].astype(F32) for source in sources]
        angle = jnp.concatenate([part[:8] + part[8:] for part in parts], axis=0)
        both = jnp.concatenate(cos_sin(angle), axis=1)
        halves = jnp.concatenate(split(both), axis=0)
        wide = lax.dot_general(
            halves, repeat, (((0,), (0,)), ((), ())), preferred_element_type=F32
        )
        cos_part, sin_part = wide[:128], wide[128:]
        weighted = jnp.concatenate([cos_part[:points] * charge, sin_part[:points] * charge], axis=1)
        weighted = weighted.astype(BF16)
        state = dot(leaf_matrix, jnp.concatenate([weighted, weighted], axis=0))
        turned = cos_part[points:angles], sin_part[points:angles]
        return [state[:, :group_columns], state[:, group_columns:]], turned

    def compute(groups, meanwhile=None):
        group_columns = 512 * len(groups)
        wheres = [flip(layer, group) for group in groups]
        sources = [where * 4 + i for where in wheres for i in range(4)]
        blocks = [pl.ds(pl.multiple_of(where * 512, 512), 512) for where in wheres]

        def table(values, start, rows):
            return jnp.concatenate(
                [values[start : start + rows, block] for block in blocks], axis=1
            )

        state_own, turn_own = leaf(own, sources)
        if meanwhile is not None:
            pass_on(meanwhile)
        for source in sources:
            across(source).wait_recv()
        state_peer, turn_peer = leaf(peer, sources)
        state = jnp.concatenate(state_own + state_peer, axis=0).astype(BF16)
        first = dot(both_matrix, state)
        first = first[: 4 * rank] + first[4 * rank :]
        own_real, own_imag = turn(first[:rank], first[rank : 2 * rank], *turn_own)
        peer_real, peer_imag = turn(first[2 * rank : 3 * rank], first[3 * rank :], *turn_peer)
        moved = jnp.concatenate(
            [
                jnp.concatenate([own_real, peer_real], axis=1),
                jnp.concatenate([own_imag, peer_imag], axis=1),
            ],
            axis=0,
        ).astype(BF16)
        middle = dot(swi_matrix, jnp.concatenate([moved, moved], axis=0))
        own_real, own_imag = turn(
            middle[:rank, :group_columns],
            middle[rank:, :group_columns],
            table(cos_table, 0, rank),
            table(sin_table, 0, rank),
        )
        peer_real, peer_imag = turn(
            middle[:rank, group_columns:],
            middle[rank:, group_columns:],
            table(cos_peer, 0, rank),
            table(sin_peer, 0, rank),
        )
        state = jnp.concatenate([own_real, own_imag, peer_real, peer_imag], axis=0).astype(BF16)
        last = dot(last_matrix, state)
        last = last[: 2 * rank] + last[2 * rank :]
        real, imag = turn(
            last[:rank],
            last[rank:],
            table(cos_table, rank, rank),
            table(sin_table, rank, rank),
        )
        high, low = split(jnp.concatenate([real, imag], axis=1))
        value = dot(out_matrix, jnp.concatenate([high, high, low], axis=0))
        result = (
            table(cos_table, 2 * rank, points) * value[:, :group_columns]
            - table(sin_table, 2 * rank, points) * value[:, group_columns:]
        ).astype(BF16)
        for i, block in enumerate(blocks):
            field[:, block] = result[:, i * 512 : (i + 1) * 512]

    pass_on(0)
    send([6, 12, 7, 13])
    local = jnp.concatenate([switch_angle[...], level_angle[1], out_angle[...]], axis=0)
    fill(local, 0, cos_table, sin_table)
    pass_on(1)
    send([14, 15])
    switch_copy.wait_recv()
    fill(peer_switch[...], 0, cos_peer, sin_peer)
    compute((0, 1), 2)
    compute((2,), 3)
    compute((3,))

    for bits in range(1, 16):
        to_wide(bits).wait_send()
    for source in range(16):
        across(source).wait_send()
    switch_copy.wait_send()


def paired_body(*operands):
    charges, leaf_angle, lagrange = operands[:3]
    points, columns = charges.shape
    rank = lagrange.shape[0]
    per_box = columns // leaf_angle.shape[1]
    operands = operands[:-1] + (operands[-1].T,)
    return pl.pallas_call(
        functools.partial(kernel, per_box),
        out_shape=pltpu.VMEM((points, columns), BF16),
        in_specs=[pl.BlockSpec(memory_space=pltpu.HBM)] * len(operands),
        out_specs=pl.BlockSpec(memory_space=pltpu.VMEM),
        scratch_shapes=[pltpu.VMEM(operand.shape, F32) for operand in operands]
        + [
            pltpu.VMEM((16, points + 16, 128), BF16),
            pltpu.VMEM((16, points + 16, 128), BF16),
            pltpu.VMEM((16, points + 16, 128), BF16),
            pltpu.VMEM((rank, 128), F32),
            pltpu.VMEM((2 * rank + points, columns), F32),
            pltpu.VMEM((2 * rank + points, columns), F32),
            pltpu.VMEM((rank, columns), F32),
            pltpu.VMEM((rank, columns), F32),
            pltpu.SemaphoreType.DMA((16,)),
            pltpu.SemaphoreType.DMA((16,)),
            pltpu.SemaphoreType.DMA((16,)),
            pltpu.SemaphoreType.DMA((16,)),
            pltpu.SemaphoreType.DMA((2,)),
            pltpu.SemaphoreType.DMA((len(operands),)),
        ],
        compiler_params=pltpu.CompilerParams(
            collective_id=0, has_side_effects=True, vmem_limit_bytes=58 * 1024 * 1024
        ),
        cost_estimate=pl.CostEstimate(
            flops=2 * 60000 * 2 * columns, bytes_accessed=4 * points * columns, transcendentals=0
        ),
    )(*operands)


def fits_pairs(mesh, charges, leaf_angle, lagrange):
    devices = mesh.shape["wide"] * mesh.shape["narrow"]
    columns = charges.shape[1] // devices
    boxes = leaf_angle.shape[1] // devices
    return (
        mesh.shape["narrow"] == 2
        and mesh.shape["wide"] == 16
        and columns == 2048
        and boxes == 128
        and charges.shape[0] % 16 == 0
        and lagrange.shape[0] % 16 == 0
        and charges.shape[0] + lagrange.shape[0] <= 128
    )


def solution(mesh):
    def program(charges, leaf_angle, lagrange, *rest):
        fits = fits_pairs(mesh, charges, leaf_angle, lagrange)
        return jax.shard_map(
            paired_body if fits else staged_body,
            mesh=mesh,
            in_specs=(
                P(None, ("wide", "narrow")),
                P(None, ("wide", "narrow")),
                P(),
                P(None, None, ("wide", "narrow")),
                P(),
                P(),
                P(None, ("wide", "narrow")),
                P(),
                P(None, ("wide", "narrow")),
                P(),
            ),
            out_specs=P(None, ("wide", "narrow")),
            check_vma=False,
        )(charges, leaf_angle, lagrange, *rest)

    return program
```

```python
import functools

import jax
import jax.numpy as jnp
from jax import lax
from jax.experimental import pallas as pl
from jax.experimental.pallas import tpu as pltpu
from jax.sharding import PartitionSpec as P

MESH = pl.DeviceIdType.MESH
F32 = jnp.float32
BF16 = jnp.bfloat16


def from_partner(value, axis, apart):
    mask = 2**apart
    pairs = [(source, source ^ mask) for source in range(lax.axis_size(axis))]
    return lax.ppermute(value, axis, pairs)


def product(left, right):
    return jnp.dot(left, right, precision=lax.Precision.HIGHEST, preferred_element_type=jnp.float32)


def rotate(boxes_state, phase_angle, per_box):
    rank = phase_angle.shape[0]
    cos_part = jnp.repeat(jnp.cos(phase_angle), per_box, axis=1)
    sin_part = jnp.repeat(jnp.sin(phase_angle), per_box, axis=1)
    real_part = boxes_state[:rank]
    imag_part = boxes_state[rank:]
    return jnp.concatenate(
        [cos_part * real_part - sin_part * imag_part, sin_part * real_part + cos_part * imag_part],
        axis=0,
    )


def butterfly_level(boxes_state, self_matrix, peer_matrix, phase_angle, bit, per_box):
    sent_state = boxes_state.astype(jnp.bfloat16)
    received = from_partner(sent_state, "narrow", bit)
    combined = product(self_matrix, boxes_state) + product(
        peer_matrix, received.astype(jnp.float32)
    )
    return rotate(combined, phase_angle, per_box)


def leaf_weights(lagrange, point_charges, point_angle, per_box):
    cos_leaf = jnp.repeat(jnp.cos(point_angle), per_box, axis=1)
    sin_leaf = jnp.repeat(jnp.sin(point_angle), per_box, axis=1)
    return jnp.concatenate(
        [product(lagrange, cos_leaf * point_charges), product(lagrange, sin_leaf * point_charges)],
        axis=0,
    )


def staged_body(
    charges,
    leaf_angle,
    lagrange,
    level_angle,
    level_self,
    level_peer,
    switch_angle,
    switch_matrix,
    out_angle,
    evaluate,
):
    per_box = charges.shape[1] // leaf_angle.shape[1]
    rank = lagrange.shape[0]
    last_bit = lax.axis_size("narrow").bit_length() - 2
    boxes_state = leaf_weights(lagrange, charges, leaf_angle, per_box)
    boxes_state = butterfly_level(
        boxes_state, level_self[0], level_peer[0], level_angle[0], 0, per_box
    )
    boxes_state = lax.all_to_all(boxes_state, "wide", split_axis=1, concat_axis=1, tiled=True)
    boxes_state = rotate(product(switch_matrix, boxes_state), switch_angle, per_box)
    boxes_state = butterfly_level(
        boxes_state, level_self[1], level_peer[1], level_angle[1], last_bit, per_box
    )
    real_part = product(evaluate, boxes_state[:rank])
    imag_part = product(evaluate, boxes_state[rank:])
    cos_out = jnp.repeat(jnp.cos(out_angle), per_box, axis=1)
    sin_out = jnp.repeat(jnp.sin(out_angle), per_box, axis=1)
    return (cos_out * real_part - sin_out * imag_part).astype(jnp.bfloat16)


def cos_sin(angle):
    half = angle * 0.5
    t = half * half
    s = half * (
        1.0
        + t * (-1 / 6 + t * (1 / 120 + t * (-1 / 5040 + t * (1 / 362880 + t * (-1 / 39916800)))))
    )
    c = 1.0 + t * (
        -1 / 2
        + t * (1 / 24 + t * (-1 / 720 + t * (1 / 40320 + t * (-1 / 3628800 + t / 479001600))))
    )
    return 1.0 - 2.0 * s * s, 2.0 * s * c


def split(value):
    high = value.astype(BF16)
    return high, (value - high.astype(F32)).astype(BF16)


def dot(left, right):
    return jnp.dot(left, right, preferred_element_type=F32)


def spread(boxes, columns, first, per_box):
    box = lax.broadcasted_iota(jnp.int32, (boxes, columns), 0)
    column = lax.broadcasted_iota(jnp.int32, (boxes, columns), 1) + first * per_box
    low = box * per_box
    once = jnp.where((column >= low) & (column < low + per_box), 1.0, 0.0).astype(BF16)
    return jnp.concatenate([once, once], axis=0)


def flip(index, bits):
    if bits == 0:
        return index
    if bits == 1:
        return index + 1 - 2 * lax.rem(index, 2)
    if bits == 2:
        return lax.rem(index + 2, 4)
    return 3 - index


def turn(real, imag, cos_part, sin_part):
    return cos_part * real - sin_part * imag, sin_part * real + cos_part * imag


def kernel(
    per_box,
    *refs,
):
    given, refs = refs[:10], refs[10:]
    field, (held, refs) = refs[0], (refs[1:11], refs[11:])
    (
        charges,
        leaf_angle,
        lagrange,
        level_angle,
        level_self,
        level_peer,
        switch_angle,
        switch_matrix,
        out_angle,
        evaluate,
    ) = held
    (
    outbox,
    own,
    peer,
    peer_switch,
    cos_table,
    sin_table,
    cos_peer,
    sin_peer,
    wide_send,
    wide_recv,
    narrow_send,
    narrow_recv,
    switch_sems,
    load_sems,
    ) = refs
    loads = [pltpu.make_async_copy(g, h, load_sems.at[i]) for i, (g, h) in enumerate(zip(given, held))]
    first_loads = [1, 3, 0, 6]
    later_loads = [i for i in range(10) if i not in first_loads]
    for i in first_loads + later_loads:
        loads[i].start()
    me = lax.axis_index("wide")
    row = lax.axis_index("narrow")
    layer = me // 4
    place = lax.rem(me, 4)
    other = 1 - row
    rank, points = lagrange.shape
    angles = points + rank

    barrier = pltpu.get_barrier_semaphore()
    for bits in range(1, 16):
        to = flip(layer, bits // 4) * 4 + flip(place, bits % 4)
        pl.semaphore_signal(barrier, inc=1, device_id={"wide": to}, device_id_type=MESH)
    pl.semaphore_signal(barrier, inc=1, device_id={"narrow": other}, device_id_type=MESH)

    for i in first_loads:
        loads[i].wait()

    stacked = jnp.concatenate(
        [leaf_angle[...], level_angle[0], jnp.zeros((128 - angles, 128), F32)], axis=0
    )
    by_box = stacked.T
    high = by_box.astype(BF16).astype(F32)
    low = by_box - high
    for to in range(16):
        outbox[to, :points, :] = charges[:, to * 128 : (to + 1) * 128].astype(BF16)
        pair = jnp.concatenate([high[to * 8 : to * 8 + 8], low[to * 8 : to * 8 + 8]], axis=0)
        outbox[to, points : points + 16, :] = pair.astype(BF16)
    own[me] = outbox[me]

    def to_wide(bits):
        to = flip(layer, bits // 4) * 4 + flip(place, bits % 4)
        return pltpu.make_async_remote_copy(
            src_ref=outbox.at[to],
            dst_ref=own.at[me],
            send_sem=wide_send.at[to],
            recv_sem=wide_recv.at[me],
            device_id={"wide": to},
            device_id_type=MESH,
        )

    def from_wide(source):
        return pltpu.make_async_remote_copy(
            src_ref=outbox.at[source],
            dst_ref=own.at[source],
            send_sem=wide_send.at[source],
            recv_sem=wide_recv.at[source],
            device_id={"wide": source},
            device_id_type=MESH,
        )

    def across(source):
        return pltpu.make_async_remote_copy(
            src_ref=own.at[source],
            dst_ref=peer.at[source],
            send_sem=narrow_send.at[source],
            recv_sem=narrow_recv.at[source],
            device_id={"narrow": other},
            device_id_type=MESH,
        )

    switch_copy = pltpu.make_async_remote_copy(
        src_ref=switch_angle,
        dst_ref=peer_switch,
        send_sem=switch_sems.at[0],
        recv_sem=switch_sems.at[1],
        device_id={"narrow": other},
        device_id_type=MESH,
    )

    pl.semaphore_wait(barrier, 16)
    order = [8, 9, 1, 10, 11, 2, 12, 4, 13, 3, 14, 5, 15, 6, 7]
    for bits in order:
        to_wide(bits).start()
    across(me).start()
    switch_copy.start()

    def pass_on(group):
        for bits in range(4):
            if group or bits:
                source = flip(layer, group) * 4 + flip(place, bits)
                from_wide(source).wait_recv()
                across(source).start()

    for i in later_loads:
        loads[i].wait()

    fill_columns = 4 * 128

    def fill(angle, first_row, cos_to, sin_to):
        rows = angle.shape[0]
        both = jnp.concatenate(cos_sin(angle), axis=0)
        halves = jnp.concatenate(split(both), axis=1)
        for group in range(4):
            columns = pl.ds(group * fill_columns, fill_columns)
            wide = dot(halves, spread(128, fill_columns, group * fill_columns // per_box, per_box))
            cos_to[pl.ds(first_row, rows), columns] = wide[:rows]
            sin_to[pl.ds(first_row, rows), columns] = wide[rows:]


    lag_high, lag_low = split(lagrange[...])
    leaf_matrix = jnp.concatenate([lag_high, lag_low], axis=1)
    eva_high, eva_low = split(evaluate[...].T)
    out_matrix = jnp.concatenate([eva_high, eva_low, eva_high], axis=1)
    both_matrix = split(
        jnp.concatenate(
            [
                jnp.concatenate([level_self[0], level_peer[0]], axis=1),
                jnp.concatenate([level_peer[0], level_self[0]], axis=1),
            ],
            axis=0,
        )
    )
    both_matrix = jnp.concatenate(both_matrix, axis=0)
    swi_high, swi_low = split(switch_matrix[...])
    swi_matrix = jnp.concatenate([swi_high, swi_low], axis=1)
    last_matrix = split(jnp.concatenate([level_self[1], level_peer[1]], axis=1))
    last_matrix = jnp.concatenate(last_matrix, axis=0)

    def leaf(box, sources):
        group_columns = 128 * len(sources)
        repeat = spread(8 * len(sources), group_columns, 0, per_box)
        charge = jnp.concatenate([box[source, :points, :] for source in sources], axis=1).astype(F32)
        parts = [box[source, points : points + 16, :].astype(F32) for source in sources]
        angle = jnp.concatenate([part[:8] + part[8:] for part in parts], axis=0)
        both = jnp.concatenate(cos_sin(angle), axis=1)
        halves = jnp.concatenate(split(both), axis=0)
        wide = lax.dot_general(
            halves, repeat, (((0,), (0,)), ((), ())), preferred_element_type=F32
        )
        cos_part, sin_part = wide[:128], wide[128:]
        weighted = jnp.concatenate([cos_part[:points] * charge, sin_part[:points] * charge], axis=1)
        weighted = weighted.astype(BF16)
        state = dot(leaf_matrix, jnp.concatenate([weighted, weighted], axis=0))
        turned = cos_part[points:angles], sin_part[points:angles]
        return [state[:, :group_columns], state[:, group_columns:]], turned

    def compute(groups, meanwhile=None):
        group_columns = 512 * len(groups)
        wheres = [flip(layer, group) for group in groups]
        sources = [where * 4 + i for where in wheres for i in range(4)]
        blocks = [pl.ds(pl.multiple_of(where * 512, 512), 512) for where in wheres]

        def table(values, start, rows):
            return jnp.concatenate(
                [values[start : start + rows, block] for block in blocks], axis=1
            )

        state_own, turn_own = leaf(own, sources)
        if meanwhile is not None:
            pass_on(meanwhile)
        for source in sources:
            across(source).wait_recv()
        state_peer, turn_peer = leaf(peer, sources)
        state = jnp.concatenate(state_own + state_peer, axis=0).astype(BF16)
        first = dot(both_matrix, state)
        first = first[: 4 * rank] + first[4 * rank :]
        own_real, own_imag = turn(first[:rank], first[rank : 2 * rank], *turn_own)
        peer_real, peer_imag = turn(first[2 * rank : 3 * rank], first[3 * rank :], *turn_peer)
        moved = jnp.concatenate(
            [
                jnp.concatenate([own_real, peer_real], axis=1),
                jnp.concatenate([own_imag, peer_imag], axis=1),
            ],
            axis=0,
        ).astype(BF16)
        middle = dot(swi_matrix, jnp.concatenate([moved, moved], axis=0))
        own_real, own_imag = turn(
            middle[:rank, :group_columns],
            middle[rank:, :group_columns],
            table(cos_table, 0, rank),
            table(sin_table, 0, rank),
        )
        peer_real, peer_imag = turn(
            middle[:rank, group_columns:],
            middle[rank:, group_columns:],
            table(cos_peer, 0, rank),
            table(sin_peer, 0, rank),
        )
        state = jnp.concatenate([own_real, own_imag, peer_real, peer_imag], axis=0).astype(BF16)
        last = dot(last_matrix, state)
        last = last[: 2 * rank] + last[2 * rank :]
        real, imag = turn(
            last[:rank],
            last[rank:],
            table(cos_table, rank, rank),
            table(sin_table, rank, rank),
        )
        high, low = split(jnp.concatenate([real, imag], axis=1))
        value = dot(out_matrix, jnp.concatenate([high, high, low], axis=0))
        result = (
            table(cos_table, 2 * rank, points) * value[:, :group_columns]
            - table(sin_table, 2 * rank, points) * value[:, group_columns:]
        ).astype(BF16)
        for i, block in enumerate(blocks):
            field[:, block] = result[:, i * 512 : (i + 1) * 512]

    pass_on(0)
    local = jnp.concatenate([switch_angle[...], level_angle[1], out_angle[...]], axis=0)
    fill(local, 0, cos_table, sin_table)
    pass_on(1)
    switch_copy.wait_recv()
    fill(peer_switch[...], 0, cos_peer, sin_peer)
    compute((0, 1), 2)
    compute((2,), 3)
    compute((3,))

    for bits in range(1, 16):
        to_wide(bits).wait_send()
    for source in range(16):
        across(source).wait_send()
    switch_copy.wait_send()


def paired_body(*operands):
    charges, leaf_angle, lagrange = operands[:3]
    points, columns = charges.shape
    rank = lagrange.shape[0]
    per_box = columns // leaf_angle.shape[1]
    operands = operands[:-1] + (operands[-1].T,)
    return pl.pallas_call(
        functools.partial(kernel, per_box),
        out_shape=pltpu.VMEM((points, columns), BF16),
        in_specs=[pl.BlockSpec(memory_space=pltpu.HBM)] * len(operands),
        out_specs=pl.BlockSpec(memory_space=pltpu.VMEM),
        scratch_shapes=[pltpu.VMEM(operand.shape, F32) for operand in operands]
        + [
            pltpu.VMEM((16, points + 16, 128), BF16),
            pltpu.VMEM((16, points + 16, 128), BF16),
            pltpu.VMEM((16, points + 16, 128), BF16),
            pltpu.VMEM((rank, 128), F32),
            pltpu.VMEM((2 * rank + points, columns), F32),
            pltpu.VMEM((2 * rank + points, columns), F32),
            pltpu.VMEM((rank, columns), F32),
            pltpu.VMEM((rank, columns), F32),
            pltpu.SemaphoreType.DMA((16,)),
            pltpu.SemaphoreType.DMA((16,)),
            pltpu.SemaphoreType.DMA((16,)),
            pltpu.SemaphoreType.DMA((16,)),
            pltpu.SemaphoreType.DMA((2,)),
            pltpu.SemaphoreType.DMA((len(operands),)),
        ],
        compiler_params=pltpu.CompilerParams(
            collective_id=0, has_side_effects=True, vmem_limit_bytes=58 * 1024 * 1024
        ),
        cost_estimate=pl.CostEstimate(
            flops=2 * 60000 * 2 * columns, bytes_accessed=4 * points * columns, transcendentals=0
        ),
    )(*operands)


def fits_pairs(mesh, charges, leaf_angle, lagrange):
    devices = mesh.shape["wide"] * mesh.shape["narrow"]
    columns = charges.shape[1] // devices
    boxes = leaf_angle.shape[1] // devices
    return (
        mesh.shape["narrow"] == 2
        and mesh.shape["wide"] == 16
        and columns == 2048
        and boxes == 128
        and charges.shape[0] % 16 == 0
        and lagrange.shape[0] % 16 == 0
        and charges.shape[0] + lagrange.shape[0] <= 128
    )


def solution(mesh):
    def program(charges, leaf_angle, lagrange, *rest):
        fits = fits_pairs(mesh, charges, leaf_angle, lagrange)
        return jax.shard_map(
            paired_body if fits else staged_body,
            mesh=mesh,
            in_specs=(
                P(None, ("wide", "narrow")),
                P(None, ("wide", "narrow")),
                P(),
                P(None, None, ("wide", "narrow")),
                P(),
                P(),
                P(None, ("wide", "narrow")),
                P(),
                P(None, ("wide", "narrow")),
                P(),
            ),
            out_specs=P(None, ("wide", "narrow")),
            check_vma=False,
        )(charges, leaf_angle, lagrange, *rest)

    return program
```

```python
import functools

import jax
import jax.numpy as jnp
from jax import lax
from jax.experimental import pallas as pl
from jax.experimental.pallas import tpu as pltpu
from jax.sharding import PartitionSpec as P

MESH = pl.DeviceIdType.MESH
F32 = jnp.float32
BF16 = jnp.bfloat16


def from_partner(value, axis, apart):
    mask = 2**apart
    pairs = [(source, source ^ mask) for source in range(lax.axis_size(axis))]
    return lax.ppermute(value, axis, pairs)


def product(left, right):
    return jnp.dot(left, right, precision=lax.Precision.HIGHEST, preferred_element_type=jnp.float32)


def rotate(boxes_state, phase_angle, per_box):
    rank = phase_angle.shape[0]
    cos_part = jnp.repeat(jnp.cos(phase_angle), per_box, axis=1)
    sin_part = jnp.repeat(jnp.sin(phase_angle), per_box, axis=1)
    real_part = boxes_state[:rank]
    imag_part = boxes_state[rank:]
    return jnp.concatenate(
        [cos_part * real_part - sin_part * imag_part, sin_part * real_part + cos_part * imag_part],
        axis=0,
    )


def butterfly_level(boxes_state, self_matrix, peer_matrix, phase_angle, bit, per_box):
    sent_state = boxes_state.astype(jnp.bfloat16)
    received = from_partner(sent_state, "narrow", bit)
    combined = product(self_matrix, boxes_state) + product(
        peer_matrix, received.astype(jnp.float32)
    )
    return rotate(combined, phase_angle, per_box)


def leaf_weights(lagrange, point_charges, point_angle, per_box):
    cos_leaf = jnp.repeat(jnp.cos(point_angle), per_box, axis=1)
    sin_leaf = jnp.repeat(jnp.sin(point_angle), per_box, axis=1)
    return jnp.concatenate(
        [product(lagrange, cos_leaf * point_charges), product(lagrange, sin_leaf * point_charges)],
        axis=0,
    )


def staged_body(
    charges,
    leaf_angle,
    lagrange,
    level_angle,
    level_self,
    level_peer,
    switch_angle,
    switch_matrix,
    out_angle,
    evaluate,
):
    per_box = charges.shape[1] // leaf_angle.shape[1]
    rank = lagrange.shape[0]
    last_bit = lax.axis_size("narrow").bit_length() - 2
    boxes_state = leaf_weights(lagrange, charges, leaf_angle, per_box)
    boxes_state = butterfly_level(
        boxes_state, level_self[0], level_peer[0], level_angle[0], 0, per_box
    )
    boxes_state = lax.all_to_all(boxes_state, "wide", split_axis=1, concat_axis=1, tiled=True)
    boxes_state = rotate(product(switch_matrix, boxes_state), switch_angle, per_box)
    boxes_state = butterfly_level(
        boxes_state, level_self[1], level_peer[1], level_angle[1], last_bit, per_box
    )
    real_part = product(evaluate, boxes_state[:rank])
    imag_part = product(evaluate, boxes_state[rank:])
    cos_out = jnp.repeat(jnp.cos(out_angle), per_box, axis=1)
    sin_out = jnp.repeat(jnp.sin(out_angle), per_box, axis=1)
    return (cos_out * real_part - sin_out * imag_part).astype(jnp.bfloat16)


def cos_sin(angle):
    half = angle * 0.5
    t = half * half
    s = half * (
        1.0
        + t * (-1 / 6 + t * (1 / 120 + t * (-1 / 5040 + t * (1 / 362880 + t * (-1 / 39916800)))))
    )
    c = 1.0 + t * (
        -1 / 2
        + t * (1 / 24 + t * (-1 / 720 + t * (1 / 40320 + t * (-1 / 3628800 + t / 479001600))))
    )
    return 1.0 - 2.0 * s * s, 2.0 * s * c


def split(value):
    high = value.astype(BF16)
    return high, (value - high.astype(F32)).astype(BF16)


def dot(left, right):
    return jnp.dot(left, right, preferred_element_type=F32)


def spread(boxes, columns, first, per_box):
    box = lax.broadcasted_iota(jnp.int32, (boxes, columns), 0)
    column = lax.broadcasted_iota(jnp.int32, (boxes, columns), 1) + first * per_box
    low = box * per_box
    once = jnp.where((column >= low) & (column < low + per_box), 1.0, 0.0).astype(BF16)
    return jnp.concatenate([once, once], axis=0)


def flip(index, bits):
    if bits == 0:
        return index
    if bits == 1:
        return index + 1 - 2 * lax.rem(index, 2)
    if bits == 2:
        return lax.rem(index + 2, 4)
    return 3 - index


def turn(real, imag, cos_part, sin_part):
    return cos_part * real - sin_part * imag, sin_part * real + cos_part * imag


def kernel(
    per_box,
    *refs,
):
    given, refs = refs[:10], refs[10:]
    field, (held, refs) = refs[0], (refs[1:11], refs[11:])
    (
        charges,
        leaf_angle,
        lagrange,
        level_angle,
        level_self,
        level_peer,
        switch_angle,
        switch_matrix,
        out_angle,
        evaluate,
    ) = held
    (
    outbox,
    own,
    peer,
    peer_switch,
    cos_table,
    sin_table,
    cos_peer,
    sin_peer,
    wide_send,
    wide_recv,
    narrow_send,
    narrow_recv,
    switch_sems,
    load_sems,
    ) = refs
    loads = [pltpu.make_async_copy(g, h, load_sems.at[i]) for i, (g, h) in enumerate(zip(given, held))]
    first_loads = [1, 3, 0, 6]
    later_loads = [i for i in range(10) if i not in first_loads]
    for i in first_loads + later_loads:
        loads[i].start()
    me = lax.axis_index("wide")
    row = lax.axis_index("narrow")
    layer = me // 4
    place = lax.rem(me, 4)
    other = 1 - row
    rank, points = lagrange.shape
    angles = points + rank

    barrier = pltpu.get_barrier_semaphore()
    for bits in range(1, 16):
        to = flip(layer, bits // 4) * 4 + flip(place, bits % 4)
        pl.semaphore_signal(barrier, inc=1, device_id={"wide": to}, device_id_type=MESH)
    pl.semaphore_signal(barrier, inc=1, device_id={"narrow": other}, device_id_type=MESH)

    for i in first_loads:
        loads[i].wait()

    stacked = jnp.concatenate(
        [leaf_angle[...], level_angle[0], jnp.zeros((128 - angles, 128), F32)], axis=0
    )
    by_box = stacked.T
    high = by_box.astype(BF16).astype(F32)
    low = by_box - high
    for to in range(16):
        outbox[to, :points, :] = charges[:, to * 128 : (to + 1) * 128].astype(BF16)
        pair = jnp.concatenate([high[to * 8 : to * 8 + 8], low[to * 8 : to * 8 + 8]], axis=0)
        outbox[to, points : points + 16, :] = pair.astype(BF16)
    own[me] = outbox[me]

    def to_wide(bits):
        to = flip(layer, bits // 4) * 4 + flip(place, bits % 4)
        return pltpu.make_async_remote_copy(
            src_ref=outbox.at[to],
            dst_ref=own.at[me],
            send_sem=wide_send.at[to],
            recv_sem=wide_recv.at[me],
            device_id={"wide": to},
            device_id_type=MESH,
        )

    def from_wide(source):
        return pltpu.make_async_remote_copy(
            src_ref=outbox.at[source],
            dst_ref=own.at[source],
            send_sem=wide_send.at[source],
            recv_sem=wide_recv.at[source],
            device_id={"wide": source},
            device_id_type=MESH,
        )

    def across(source):
        return pltpu.make_async_remote_copy(
            src_ref=own.at[source],
            dst_ref=peer.at[source],
            send_sem=narrow_send.at[source],
            recv_sem=narrow_recv.at[source],
            device_id={"narrow": other},
            device_id_type=MESH,
        )

    switch_copy = pltpu.make_async_remote_copy(
        src_ref=switch_angle,
        dst_ref=peer_switch,
        send_sem=switch_sems.at[0],
        recv_sem=switch_sems.at[1],
        device_id={"narrow": other},
        device_id_type=MESH,
    )

    pl.semaphore_wait(barrier, 16)
    across(me).start()
    order = [1, 8, 2, 9, 4, 10, 3, 11, 5, 12, 6, 13, 7, 14, 15]
    for bits in order:
        to_wide(bits).start()
    switch_copy.start()

    def pass_on(group):
        for bits in range(4):
            if group or bits:
                source = flip(layer, group) * 4 + flip(place, bits)
                from_wide(source).wait_recv()
                across(source).start()

    for i in later_loads:
        loads[i].wait()

    fill_columns = 4 * 128

    def fill(angle, first_row, cos_to, sin_to):
        rows = angle.shape[0]
        both = jnp.concatenate(cos_sin(angle), axis=0)
        halves = jnp.concatenate(split(both), axis=1)
        for group in range(4):
            columns = pl.ds(group * fill_columns, fill_columns)
            wide = dot(halves, spread(128, fill_columns, group * fill_columns // per_box, per_box))
            cos_to[pl.ds(first_row, rows), columns] = wide[:rows]
            sin_to[pl.ds(first_row, rows), columns] = wide[rows:]


    lag_high, lag_low = split(lagrange[...])
    leaf_matrix = jnp.concatenate([lag_high, lag_low], axis=1)
    eva_high, eva_low = split(evaluate[...].T)
    out_matrix = jnp.concatenate([eva_high, eva_low, eva_high], axis=1)
    both_matrix = split(
        jnp.concatenate(
            [
                jnp.concatenate([level_self[0], level_peer[0]], axis=1),
                jnp.concatenate([level_peer[0], level_self[0]], axis=1),
            ],
            axis=0,
        )
    )
    both_matrix = jnp.concatenate(both_matrix, axis=1)
    swi_high, swi_low = split(switch_matrix[...])
    swi_matrix = jnp.concatenate([swi_high, swi_low], axis=1)
    last_matrix = split(jnp.concatenate([level_self[1], level_peer[1]], axis=1))
    last_matrix = jnp.concatenate(last_matrix, axis=1)

    def leaf(box, sources):
        group_columns = 128 * len(sources)
        repeat = spread(8 * len(sources), group_columns, 0, per_box)
        charge = jnp.concatenate([box[source, :points, :] for source in sources], axis=1).astype(F32)
        parts = [box[source, points : points + 16, :].astype(F32) for source in sources]
        angle = jnp.concatenate([part[:8] + part[8:] for part in parts], axis=0)
        both = jnp.concatenate(cos_sin(angle), axis=1)
        halves = jnp.concatenate(split(both), axis=0)
        wide = lax.dot_general(
            halves, repeat, (((0,), (0,)), ((), ())), preferred_element_type=F32
        )
        cos_part, sin_part = wide[:128], wide[128:]
        weighted = jnp.concatenate([cos_part[:points] * charge, sin_part[:points] * charge], axis=1)
        weighted = weighted.astype(BF16)
        state = dot(leaf_matrix, jnp.concatenate([weighted, weighted], axis=0))
        turned = cos_part[points:angles], sin_part[points:angles]
        return [state[:, :group_columns], state[:, group_columns:]], turned

    def compute(groups, meanwhile=None):
        group_columns = 512 * len(groups)
        wheres = [flip(layer, group) for group in groups]
        sources = [where * 4 + i for where in wheres for i in range(4)]
        blocks = [pl.ds(pl.multiple_of(where * 512, 512), 512) for where in wheres]

        def table(values, start, rows):
            return jnp.concatenate(
                [values[start : start + rows, block] for block in blocks], axis=1
            )

        state_own, turn_own = leaf(own, sources)
        if meanwhile is not None:
            pass_on(meanwhile)
        for source in sources:
            across(source).wait_recv()
        state_peer, turn_peer = leaf(peer, sources)
        state = jnp.concatenate(state_own + state_peer, axis=0).astype(BF16)
        first = dot(both_matrix, jnp.concatenate([state, state], axis=0))
        own_real, own_imag = turn(first[:rank], first[rank : 2 * rank], *turn_own)
        peer_real, peer_imag = turn(first[2 * rank : 3 * rank], first[3 * rank :], *turn_peer)
        moved = jnp.concatenate(
            [
                jnp.concatenate([own_real, peer_real], axis=1),
                jnp.concatenate([own_imag, peer_imag], axis=1),
            ],
            axis=0,
        ).astype(BF16)
        middle = dot(swi_matrix, jnp.concatenate([moved, moved], axis=0))
        own_real, own_imag = turn(
            middle[:rank, :group_columns],
            middle[rank:, :group_columns],
            table(cos_table, 0, rank),
            table(sin_table, 0, rank),
        )
        peer_real, peer_imag = turn(
            middle[:rank, group_columns:],
            middle[rank:, group_columns:],
            table(cos_peer, 0, rank),
            table(sin_peer, 0, rank),
        )
        state = jnp.concatenate([own_real, own_imag, peer_real, peer_imag], axis=0).astype(BF16)
        last = dot(last_matrix, jnp.concatenate([state, state], axis=0))
        real, imag = turn(
            last[:rank],
            last[rank:],
            table(cos_table, rank, rank),
            table(sin_table, rank, rank),
        )
        high, low = split(jnp.concatenate([real, imag], axis=1))
        value = dot(out_matrix, jnp.concatenate([high, high, low], axis=0))
        result = (
            table(cos_table, 2 * rank, points) * value[:, :group_columns]
            - table(sin_table, 2 * rank, points) * value[:, group_columns:]
        ).astype(BF16)
        for i, block in enumerate(blocks):
            field[:, block] = result[:, i * 512 : (i + 1) * 512]

    pass_on(0)
    local = jnp.concatenate([switch_angle[...], level_angle[1], out_angle[...]], axis=0)
    fill(local, 0, cos_table, sin_table)
    pass_on(1)
    switch_copy.wait_recv()
    fill(peer_switch[...], 0, cos_peer, sin_peer)
    compute((0, 1), 2)
    compute((2,), 3)
    compute((3,))

    for bits in range(1, 16):
        to_wide(bits).wait_send()
    for source in range(16):
        across(source).wait_send()
    switch_copy.wait_send()


def paired_body(*operands):
    charges, leaf_angle, lagrange = operands[:3]
    points, columns = charges.shape
    rank = lagrange.shape[0]
    per_box = columns // leaf_angle.shape[1]
    operands = operands[:-1] + (operands[-1].T,)
    return pl.pallas_call(
        functools.partial(kernel, per_box),
        out_shape=pltpu.VMEM((points, columns), BF16),
        in_specs=[pl.BlockSpec(memory_space=pltpu.HBM)] * len(operands),
        out_specs=pl.BlockSpec(memory_space=pltpu.VMEM),
        scratch_shapes=[pltpu.VMEM(operand.shape, F32) for operand in operands]
        + [
            pltpu.VMEM((16, points + 16, 128), BF16),
            pltpu.VMEM((16, points + 16, 128), BF16),
            pltpu.VMEM((16, points + 16, 128), BF16),
            pltpu.VMEM((rank, 128), F32),
            pltpu.VMEM((2 * rank + points, columns), F32),
            pltpu.VMEM((2 * rank + points, columns), F32),
            pltpu.VMEM((rank, columns), F32),
            pltpu.VMEM((rank, columns), F32),
            pltpu.SemaphoreType.DMA((16,)),
            pltpu.SemaphoreType.DMA((16,)),
            pltpu.SemaphoreType.DMA((16,)),
            pltpu.SemaphoreType.DMA((16,)),
            pltpu.SemaphoreType.DMA((2,)),
            pltpu.SemaphoreType.DMA((len(operands),)),
        ],
        compiler_params=pltpu.CompilerParams(
            collective_id=0, has_side_effects=True, vmem_limit_bytes=58 * 1024 * 1024
        ),
        cost_estimate=pl.CostEstimate(
            flops=2 * 60000 * 2 * columns, bytes_accessed=4 * points * columns, transcendentals=0
        ),
    )(*operands)


def fits_pairs(mesh, charges, leaf_angle, lagrange):
    devices = mesh.shape["wide"] * mesh.shape["narrow"]
    columns = charges.shape[1] // devices
    boxes = leaf_angle.shape[1] // devices
    return (
        mesh.shape["narrow"] == 2
        and mesh.shape["wide"] == 16
        and columns == 2048
        and boxes == 128
        and charges.shape[0] % 16 == 0
        and lagrange.shape[0] % 16 == 0
        and charges.shape[0] + lagrange.shape[0] <= 128
    )


def solution(mesh):
    def program(charges, leaf_angle, lagrange, *rest):
        fits = fits_pairs(mesh, charges, leaf_angle, lagrange)
        return jax.shard_map(
            paired_body if fits else staged_body,
            mesh=mesh,
            in_specs=(
                P(None, ("wide", "narrow")),
                P(None, ("wide", "narrow")),
                P(),
                P(None, None, ("wide", "narrow")),
                P(),
                P(),
                P(None, ("wide", "narrow")),
                P(),
                P(None, ("wide", "narrow")),
                P(),
            ),
            out_specs=P(None, ("wide", "narrow")),
            check_vma=False,
        )(charges, leaf_angle, lagrange, *rest)

    return program
```
